512 devices in a mesh: dom: 64 (over x, z), rep: 8 (over y, core).
Axes of the slice: x: 4, y: 4, z: 16, core: 2. Of those that a mesh axis runs over, the one named last changes fastest.
Arguments:
- history: bfloat16 [2, 524288, 256], P(None, ('dom', 'rep')), may hold values from -6 to 6
- tile_values: bfloat16 [4096, 8, 128, 128], P(('dom', 'rep')), may hold values from -0.5 to 0.5
- tile_cols: int32 [4096, 8], P(('dom', 'rep')), may hold values from 0 to 11, all different within a row
- send_rows: int32 [512, 64, 8], P(('dom', 'rep')), may hold values from 0 to 1023
- send_count: int32 [512, 64], P(('dom', 'rep')), may hold values from 1 to 8, as said below
- node_ids: int32 [512, 1024], P(('dom', 'rep')), may hold values from 0 to 1023, each once within a row
- weights: bfloat16 [2, 256, 256], replicated, may hold values from -0.375 to 0.375
- upstream: bfloat16 [524288, 256], P(('dom', 'rep'))
Outputs:
- history_out: bfloat16 [1, 524288, 256], P(None, ('dom', 'rep'))
- weight_grads: float32 [2, 256, 256], replicated
The draws below stay inside these ranges and needn't reach their ends.
Inputs may be any that keep to these rules, and one draw needn't show every extreme that they name: In each list the first send_count entries are live and the rest empty; in every draw each device has a list of 8 live entries. `tile_cols`: each row block names 8 different column blocks; blocks below 8 hold batch rows, the others halo slots.
All inputs are finite; a program needn't handle non-finite values.
Results may differ from the reference program's by a relative error of at most 0.0065.
Values may be sent and summed in bfloat16 or wider, within the bound.
A program may use at most 64 MiB of HBM per device.

```python
import math
import jax
import jax.numpy as jnp
from jax import lax

F = 256
LAYERS = 2
TILE = 128
TILES = 8
BATCH = 1024
CAP = 8
RB = 8
NCB = 12
NODES = 524288
N_DOM = 64
N_REP = 8
DEVICES = 512


def draw_send_count(key, part):
    key = jax.random.fold_in(key, 11)
    first, second = jax.random.split(key)
    counts = jax.random.randint(first, (DEVICES, N_DOM), 1, CAP + 1)
    chosen = jax.random.randint(second, (DEVICES, 1), 0, N_DOM)
    column = jnp.arange(N_DOM, dtype=jnp.int32)[None, :]
    return jnp.where(column == chosen, CAP, counts).astype(jnp.int32)


def draw_upstream(key, part):
    key = jax.random.fold_in(key, 23)
    first = jax.random.fold_in(key, 0)
    ramp = 10.0 ** (jnp.arange(NODES, dtype=jnp.float32) / NODES)
    base = jax.random.normal(first, (NODES, F), jnp.float32)
    return (0.3 * base * ramp[:, None]).astype(jnp.bfloat16)


def set_ends(array, key, low, high):
    longest = array.shape.index(max(array.shape))
    spots = []
    for shift in (0, 1):
        where = [jax.random.randint(jax.random.fold_in(key, axis), (), 0, length) for axis, length in enumerate(array.shape)]
        where[longest] = (where[longest] + shift) % array.shape[longest]
        spots.append(tuple(where))
    return array.at[spots[0]].set(low).at[spots[1]].set(high)


def steps_of(stream_key, shape, cuts, low, high):
    loudness, own = 1.0, jax.random.fold_in(stream_key, 6)
    for axis_at, parts in cuts:
        steps = jnp.exp(jax.random.uniform(jax.random.fold_in(own, axis_at), (parts,), jnp.float32, low / len(cuts), high / len(cuts)))
        loudness = loudness * jnp.repeat(steps, shape[axis_at] // parts).reshape([-1 if axis == axis_at else 1 for axis in range(len(shape))])
    return loudness


def distinct(key, rows, number_of, top, lift):
    ranking = jax.random.permutation(jax.random.fold_in(key, 1), number_of)
    boost = ranking
    for power in range(3):
        boost = boost * boost // number_of
    boost = boost * lift // number_of
    tickets = jax.random.randint(jax.random.fold_in(key, 2), (rows, number_of), 0, 4096) + boost
    holders = jax.random.permutation(jax.random.fold_in(key, 3), rows)[jnp.arange(number_of) % rows]
    tickets = jnp.where(jnp.arange(rows)[:, None] == holders[None, :], 1 << 14, tickets)
    score = tickets * number_of + jnp.arange(number_of)
    return lax.top_k(score.astype(jnp.int32), top)[1].astype(jnp.int32)


def normal_values(key, shape, deviation, bound, cuts=(), kind=jnp.bfloat16):
    drawn = jax.random.normal(key, shape, jnp.float32) * deviation
    if len(cuts) > 0:
        drawn = steps_of(key, shape, cuts, -0.22, 0.18) * drawn
    return jnp.clip(drawn, min=-bound, max=bound).astype(kind)


def setup_inputs(seed: int = 0) -> dict:
    key_of = jax.random.split(jax.random.key(seed), 9)
    return {
        "history": normal_values(key_of[0], (LAYERS, NODES, F), 1.0, 6.0, ((1, 512),)),
        "tile_values": normal_values(key_of[1], (NODES // TILE, TILES, TILE, TILE), ((TILES * TILE) ** -0.5), 0.5, ((0, 512),)),
        "tile_cols": distinct(key_of[2], (NODES // TILE), NCB, TILES, 0),
        "send_rows": set_ends(jax.random.randint(key_of[3], (DEVICES, N_DOM, CAP), 0, BATCH), jax.random.fold_in(key_of[3], 1), 0, BATCH - 1).astype(jnp.int32),
        "send_count": draw_send_count(jax.random.fold_in(key_of[8], 71), 0),
        "node_ids": jax.vmap(lambda own: jax.random.permutation(own, BATCH))(jax.random.split(key_of[5], DEVICES)).reshape((DEVICES, BATCH)).astype(jnp.int32),
        "weights": normal_values(key_of[6], (LAYERS, F, F), F ** -0.5, 0.375),
        "upstream": draw_upstream(jax.random.fold_in(key_of[8], 71), 0),
    }


RESTART = 0.1

def layer_beta(level):
    return math.log(0.5 / (level + 1) + 1.0)

def silu_slope(preact):
    sigma = jax.nn.sigmoid(preact)
    return sigma * (1.0 + preact * (1.0 - sigma))

def aggregate(tiles, tile_cols, node_table):
    tile_size = tiles.shape[2]
    blocks = node_table.reshape(-1, tile_size, node_table.shape[1])
    picked = blocks[tile_cols]
    summed = jnp.einsum('rtij,rtjf->rif', tiles.astype(jnp.float32), picked.astype(jnp.float32), precision=lax.Precision.HIGHEST)
    return summed.reshape(-1, node_table.shape[1])

def spread_back(tiles, tile_cols, back_rows, batch_rows):
    tile_size = tiles.shape[2]
    blocks = back_rows.reshape(-1, tile_size, back_rows.shape[1]).astype(jnp.float32)
    pieces = jnp.einsum('rtij,rif->rtjf', tiles.astype(jnp.float32), blocks, precision=lax.Precision.HIGHEST)
    targets = jnp.arange(batch_rows // tile_size, dtype=jnp.int32)
    owners = (tile_cols[:, :, None] == targets[None, None, :]).astype(jnp.float32)
    placed = jnp.einsum('rtc,rtjf->cjf', owners, pieces, precision=lax.Precision.HIGHEST)
    return placed.reshape(batch_rows, back_rows.shape[1])

def reference(history, tile_values, tile_cols, send_rows, send_count, node_ids, weights, upstream):
    block_hist = history.reshape(LAYERS, DEVICES, BATCH, F)
    tiles_all = tile_values.reshape(DEVICES, RB, TILES, TILE, TILE)
    cols_all = tile_cols.reshape(DEVICES, RB, TILES)
    upstream_all = upstream.reshape(DEVICES, BATCH, F)

    def per_device(total, device):
        dom_index = device // N_REP
        rep_index = device % N_REP
        owners = jnp.arange(N_DOM, dtype=jnp.int32) * N_REP + rep_index
        listed = send_rows[owners, dom_index]
        counts = send_count[owners, dom_index]
        live_mask = jnp.arange(CAP, dtype=jnp.int32)[None, :] < counts[:, None]
        tiles = tiles_all[device]
        cols = cols_all[device]
        node_rows = node_ids[device]
        h_start = block_hist[0, device][node_rows]
        current = h_start
        mixed_all = []
        preact_all = []
        written = []
        for level in range(LAYERS):
            picked = block_hist[level][owners[:, None], listed]
            halo_rows = jnp.where(live_mask[:, :, None], picked, jnp.zeros_like(picked)).reshape(-1, F)
            node_table = jnp.concatenate([current, halo_rows], axis=0)
            summed = aggregate(tiles, cols, node_table)
            mixed_rows = ((1.0 - RESTART) * summed + RESTART * h_start.astype(jnp.float32)).astype(jnp.bfloat16)
            beta_value = layer_beta(level)
            preact = (1.0 - beta_value) * mixed_rows.astype(jnp.float32) + beta_value * jnp.dot(mixed_rows, weights[level], preferred_element_type=jnp.float32)
            current = jax.nn.silu(preact).astype(jnp.bfloat16)
            mixed_all.append(mixed_rows)
            preact_all.append(preact)
            if level + 1 < LAYERS:
                written.append(jnp.zeros((BATCH, F), jnp.bfloat16).at[node_rows].set(current))
        grads = [None] * LAYERS
        grad_rows = (upstream_all[device].astype(jnp.float32) * silu_slope(preact_all[-1])).astype(jnp.bfloat16)
        for level in reversed(range(LAYERS)):
            beta_value = layer_beta(level)
            grads[level] = beta_value * jnp.dot(mixed_all[level].T, grad_rows, preferred_element_type=jnp.float32)
            if level > 0:
                back_rows = ((1.0 - beta_value) * grad_rows.astype(jnp.float32) + beta_value * jnp.dot(grad_rows, weights[level].T, preferred_element_type=jnp.float32)).astype(jnp.bfloat16)
                delta = (1.0 - RESTART) * spread_back(tiles, cols, back_rows, BATCH)
                grad_rows = (delta * silu_slope(preact_all[level - 1])).astype(jnp.bfloat16)
        return (total + jnp.stack(grads), jnp.stack(written))
    total, written = lax.scan(per_device, jnp.zeros((LAYERS, F, F), jnp.float32), jnp.arange(DEVICES, dtype=jnp.int32))
    history_out = jnp.transpose(written, (1, 0, 2, 3)).reshape(LAYERS - 1, NODES, F)
    return (history_out, total * (1.0 / math.sqrt(NODES)))
```

```python
import functools
import math

import jax
import jax.numpy as jnp
from jax import lax
from jax.experimental import pallas as pl
from jax.experimental.pallas import tpu as pltpu
from jax.sharding import PartitionSpec as P

RESTART = 0.1
RING = 16


def layer_beta(level):
    return math.log(0.5 / (level + 1) + 1.0)


def silu_slope(preact):
    sigma = jax.nn.sigmoid(preact)
    return sigma * (1.0 + preact * (1.0 - sigma))


def outgoing(layer_table, send_rows, send_count):
    picked = jnp.take(layer_table, send_rows[0], axis=0)
    slot_index = lax.broadcasted_iota(jnp.int32, send_rows.shape[1:], 1)
    live_mask = slot_index < send_count[0][:, None]
    return jnp.where(live_mask[:, :, None], picked, jnp.zeros_like(picked))


def aggregate(tiles, tile_cols, node_table):
    tile_size = tiles.shape[2]
    blocks = node_table.reshape(-1, tile_size, node_table.shape[1])
    picked = jnp.take(blocks, tile_cols, axis=0)
    summed = jnp.einsum("rtij,rtjf->rif", tiles, picked, preferred_element_type=jnp.float32)
    return summed.reshape(-1, node_table.shape[1])


def spread_back(tiles, tile_cols, back_rows, batch_rows):
    tile_size = tiles.shape[2]
    blocks = back_rows.reshape(-1, tile_size, back_rows.shape[1])
    pieces = jnp.einsum("rtij,rif->rtjf", tiles, blocks, preferred_element_type=jnp.float32)
    targets = lax.broadcasted_iota(jnp.int32, (1, 1, batch_rows // tile_size), 2)
    owners = (tile_cols[:, :, None] == targets).astype(jnp.float32)
    placed = jnp.einsum("rtc,rtjf->cjf", owners, pieces, precision=lax.Precision.HIGHEST)
    return placed.reshape(batch_rows, back_rows.shape[1])


MESH = pl.DeviceIdType.MESH


def span_wait(ref, sem):
    pltpu.make_async_copy(ref, ref, sem).wait()


def place(grid):
    nx, ny, nz = grid
    dom, rep = lax.axis_index("dom"), lax.axis_index("rep")
    return dom // nz, dom % nz, rep // 2, rep % 2


def plane_peer(grid, step):
    nx, ny, nz = grid
    x, z, y, core = place(grid)
    other = (x * ny + y + step) % (nx * ny)
    return ((other // ny) * nz + z, (other % ny) * 2 + core), other


def ring_peer(grid, step):
    nx, ny, nz = grid
    x, z, y, core = place(grid)
    other = (z + step) % nz
    return (x * nz + other, y * 2 + core), other


def greet_sum_peers(grid, barrier):
    nx, ny, nz = grid
    x, z, y, core = place(grid)

    def signal(target):
        pl.semaphore_signal(barrier, inc=1, device_id=target, device_id_type=MESH)

    signal((x * nz + z, y * 2 + 1 - core))
    lax.fori_loop(1, nx * ny, lambda step, c: (signal(plane_peer(grid, step)[0]), c)[1], 0)
    lax.fori_loop(1, nz, lambda step, c: (signal(ring_peer(grid, step)[0]), c)[1], 0)


def sum_body(grid, scale, grads, out, pair_src, pair_got, plane_src, plane_got, ring_src, ring_got, ring_all, plane_all, send_sems, recv_sems):
    nx, ny, nz = grid
    planes = nx * ny
    x, z, y, core = place(grid)
    partner = (x * nz + z, y * 2 + 1 - core)
    mine = x * ny + y
    rows = grads.shape[1] // planes
    piece = rows // nz

    def copy(stage, src, dst, target):
        return pltpu.make_async_remote_copy(
            src_ref=src, dst_ref=dst, send_sem=send_sems.at[stage], recv_sem=recv_sems.at[stage], device_id=target, device_id_type=MESH
        )

    pair_src[...] = grads[1 - core].astype(jnp.bfloat16)
    hop = copy(0, pair_src, pair_got, partner)
    hop.start()
    hop.wait_recv()
    plane_src[...] = (grads[core] + pair_got[...].astype(jnp.float32)).astype(jnp.bfloat16)

    def plane_send(step, c):
        target, other = plane_peer(grid, step)
        start = pl.multiple_of(other * rows, rows)
        copy(1, plane_src.at[pl.ds(start, rows)], plane_got.at[step - 1], target).start()
        return c

    lax.fori_loop(1, planes, plane_send, 0)
    own = pl.multiple_of(mine * rows, rows)
    total = grads[core, pl.ds(own, rows), :] + pair_got[pl.ds(own, rows), :].astype(jnp.float32)
    span_wait(plane_got, recv_sems.at[1])
    total = total + jnp.sum(plane_got[...].astype(jnp.float32), axis=0)
    for part in range(nz):
        ring_src[part] = total[part * piece : (part + 1) * piece]

    def ring_send(step, c):
        target, other = ring_peer(grid, step)
        copy(2, ring_src.at[other], ring_got.at[step - 1], target).start()
        return c

    lax.fori_loop(1, nz, ring_send, 0)
    part_sum = ring_src[z]
    span_wait(ring_got, recv_sems.at[2])
    for part in range(nz - 1):
        part_sum = part_sum + ring_got[part]
    ring_all[z] = part_sum * scale

    def ring_share(step, c):
        target, other = ring_peer(grid, step)
        copy(3, ring_all.at[z], ring_all.at[z], target).start()
        return c

    lax.fori_loop(1, nz, ring_share, 0)
    span_wait(ring_got, recv_sems.at[3])
    summed = jnp.concatenate([ring_all[part] for part in range(nz)], axis=0)
    plane_all[pl.ds(own, rows), :] = summed.astype(jnp.bfloat16)

    def plane_share(step, c):
        target, other = plane_peer(grid, step)
        copy(4, plane_all.at[pl.ds(own, rows)], plane_all.at[pl.ds(own, rows)], target).start()
        return c

    lax.fori_loop(1, planes, plane_share, 0)
    span_wait(plane_got, recv_sems.at[4])
    back = copy(5, plane_all, out.at[core], partner)
    back.start()
    out[core] = plane_all[...]
    back.wait_recv()
    hop.wait_send()
    span_wait(plane_got, send_sems.at[1])
    span_wait(ring_got, send_sems.at[2])
    span_wait(ring_got, send_sems.at[3])
    span_wait(plane_got, send_sems.at[4])
    back.wait_send()


def sum_scratch(grid, side):
    nx, ny, nz = grid
    planes = nx * ny
    rows = side // planes
    piece = rows // nz
    return [
        pltpu.VMEM((side, side), jnp.bfloat16),
        pltpu.VMEM((side, side), jnp.bfloat16),
        pltpu.VMEM((side, side), jnp.bfloat16),
        pltpu.VMEM((planes - 1, rows, side), jnp.bfloat16),
        pltpu.VMEM((nz, piece, side), jnp.float32),
        pltpu.VMEM((nz - 1, piece, side), jnp.float32),
        pltpu.VMEM((nz, piece, side), jnp.float32),
        pltpu.VMEM((side, side), jnp.bfloat16),
        pltpu.SemaphoreType.DMA((6,)),
        pltpu.SemaphoreType.DMA((6,)),
    ]


def all_sum(grads, grid, scale):
    nx, ny, nz = grid

    def kernel(grads_ref, out_ref, *scratch):
        barrier = pltpu.get_barrier_semaphore()
        greet_sum_peers(grid, barrier)
        pl.semaphore_wait(barrier, 1 + (nx * ny - 1) + (nz - 1))
        sum_body(grid, scale, grads_ref, out_ref, *scratch)

    return pl.pallas_call(
        kernel,
        out_shape=jax.ShapeDtypeStruct(grads.shape, jnp.bfloat16),
        in_specs=[pl.BlockSpec(memory_space=pltpu.VMEM)],
        out_specs=pl.BlockSpec(memory_space=pltpu.VMEM),
        scratch_shapes=sum_scratch(grid, grads.shape[2]),
        compiler_params=pltpu.CompilerParams(collective_id=0, has_side_effects=True),
    )(grads)


def local(grid, history, tile_values, tile_cols, send_rows, send_count, node_ids, weights, upstream):
    levels = history.shape[0]
    batch_rows = history.shape[1]
    feature_width = history.shape[2]
    node_rows = node_ids[0]
    h_start = jnp.take(history[0], node_rows, axis=0)
    halos = [
        lax.all_to_all(
            outgoing(history[level], send_rows, send_count),
            "dom",
            split_axis=0,
            concat_axis=0,
            tiled=True,
        ).reshape(-1, feature_width)
        for level in range(levels)
    ]
    current = h_start
    mixed_all = []
    preact_all = []
    written = []
    for level in range(levels):
        node_table = jnp.concatenate([current, halos[level]], axis=0)
        summed = aggregate(tile_values, tile_cols, node_table)
        mixed_rows = ((1.0 - RESTART) * summed + RESTART * h_start.astype(jnp.float32)).astype(
            jnp.bfloat16
        )
        beta_value = layer_beta(level)
        preact = (1.0 - beta_value) * mixed_rows.astype(jnp.float32) + beta_value * jnp.dot(
            mixed_rows, weights[level], preferred_element_type=jnp.float32
        )
        current = jax.nn.silu(preact).astype(jnp.bfloat16)
        mixed_all.append(mixed_rows)
        preact_all.append(preact)
        if level + 1 < levels:
            written.append(
                jnp.zeros((batch_rows, feature_width), jnp.bfloat16).at[node_rows].set(current)
            )
    grads = [None] * levels
    grad_rows = (upstream.astype(jnp.float32) * silu_slope(preact_all[-1])).astype(jnp.bfloat16)
    for level in reversed(range(levels)):
        beta_value = layer_beta(level)
        local_grad = beta_value * jnp.dot(
            mixed_all[level].T, grad_rows, preferred_element_type=jnp.float32
        )
        grads[level] = local_grad
        if level > 0:
            back_rows = (
                (1.0 - beta_value) * grad_rows.astype(jnp.float32)
                + beta_value
                * jnp.dot(grad_rows, weights[level].T, preferred_element_type=jnp.float32)
            ).astype(jnp.bfloat16)
            delta = (1.0 - RESTART) * spread_back(tile_values, tile_cols, back_rows, batch_rows)
            grad_rows = (delta * silu_slope(preact_all[level - 1])).astype(jnp.bfloat16)
    stacked = jnp.stack(grads)
    nodes_all = batch_rows * lax.axis_size("dom") * lax.axis_size("rep")
    total = all_sum(stacked, grid, 1.0 / math.sqrt(nodes_all))
    return (jnp.stack(written), total.astype(jnp.float32))


def solution(mesh):
    dom, rep = mesh.shape["dom"], mesh.shape["rep"]
    grid = (dom // RING, rep // 2, RING)
    return jax.shard_map(
        functools.partial(local, grid),
        mesh=mesh,
        in_specs=(
            P(None, ("dom", "rep"), None),
            P(("dom", "rep"), None, None, None),
            P(("dom", "rep"), None),
            P(("dom", "rep"), None, None),
            P(("dom", "rep"), None),
            P(("dom", "rep"), None),
            P(),
            P(("dom", "rep"), None),
        ),
        out_specs=(P(None, ("dom", "rep"), None), P()),
        check_vma=False,
    )
```

```python
import functools
import math

import jax
import jax.numpy as jnp
from jax import lax
from jax.experimental import pallas as pl
from jax.experimental.pallas import tpu as pltpu
from jax.sharding import PartitionSpec as P

RESTART = 0.1
RING = 16


def layer_beta(level):
    return math.log(0.5 / (level + 1) + 1.0)


def silu_slope(preact):
    sigma = jax.nn.sigmoid(preact)
    return sigma * (1.0 + preact * (1.0 - sigma))


MESH = pl.DeviceIdType.MESH


def span_wait(ref, sem):
    pltpu.make_async_copy(ref, ref, sem).wait()


def place(grid):
    nx, ny, nz = grid
    dom, rep = lax.axis_index("dom"), lax.axis_index("rep")
    return dom // nz, dom % nz, rep // 2, rep % 2


def plane_peer(grid, step):
    nx, ny, nz = grid
    x, z, y, core = place(grid)
    other = (x * ny + y + step) % (nx * ny)
    return ((other // ny) * nz + z, (other % ny) * 2 + core), other


def ring_peer(grid, step):
    nx, ny, nz = grid
    x, z, y, core = place(grid)
    other = (z + step) % nz
    return (x * nz + other, y * 2 + core), other


def greet_sum_peers(grid, barrier):
    nx, ny, nz = grid
    x, z, y, core = place(grid)

    def signal(target):
        pl.semaphore_signal(barrier, inc=1, device_id=target, device_id_type=MESH)

    signal((x * nz + z, y * 2 + 1 - core))
    lax.fori_loop(1, nx * ny, lambda step, c: (signal(plane_peer(grid, step)[0]), c)[1], 0)
    lax.fori_loop(1, nz, lambda step, c: (signal(ring_peer(grid, step)[0]), c)[1], 0)


def sum_body(grid, scale, grads, out, pair_src, pair_got, plane_src, plane_got, ring_src, ring_got, ring_all, plane_all, send_sems, recv_sems):
    nx, ny, nz = grid
    planes = nx * ny
    x, z, y, core = place(grid)
    partner = (x * nz + z, y * 2 + 1 - core)
    mine = x * ny + y
    rows = grads.shape[1] // planes
    piece = rows // nz

    def copy(stage, src, dst, target):
        return pltpu.make_async_remote_copy(
            src_ref=src, dst_ref=dst, send_sem=send_sems.at[stage], recv_sem=recv_sems.at[stage], device_id=target, device_id_type=MESH
        )

    pair_src[...] = grads[1 - core].astype(jnp.bfloat16)
    hop = copy(0, pair_src, pair_got, partner)
    hop.start()
    hop.wait_recv()
    plane_src[...] = (grads[core] + pair_got[...].astype(jnp.float32)).astype(jnp.bfloat16)

    def plane_send(step, c):
        target, other = plane_peer(grid, step)
        start = pl.multiple_of(other * rows, rows)
        copy(1, plane_src.at[pl.ds(start, rows)], plane_got.at[step - 1], target).start()
        return c

    lax.fori_loop(1, planes, plane_send, 0)
    own = pl.multiple_of(mine * rows, rows)
    total = grads[core, pl.ds(own, rows), :] + pair_got[pl.ds(own, rows), :].astype(jnp.float32)
    span_wait(plane_got, recv_sems.at[1])
    total = total + jnp.sum(plane_got[...].astype(jnp.float32), axis=0)
    for part in range(nz):
        ring_src[part] = total[part * piece : (part + 1) * piece]

    def ring_send(step, c):
        target, other = ring_peer(grid, step)
        copy(2, ring_src.at[other], ring_got.at[step - 1], target).start()
        return c

    lax.fori_loop(1, nz, ring_send, 0)
    part_sum = ring_src[z]
    span_wait(ring_got, recv_sems.at[2])
    for part in range(nz - 1):
        part_sum = part_sum + ring_got[part]
    ring_all[z] = part_sum * scale

    def ring_share(step, c):
        target, other = ring_peer(grid, step)
        copy(3, ring_all.at[z], ring_all.at[z], target).start()
        return c

    lax.fori_loop(1, nz, ring_share, 0)
    span_wait(ring_got, recv_sems.at[3])
    summed = jnp.concatenate([ring_all[part] for part in range(nz)], axis=0)
    plane_all[pl.ds(own, rows), :] = summed.astype(jnp.bfloat16)

    def plane_share(step, c):
        target, other = plane_peer(grid, step)
        copy(4, plane_all.at[pl.ds(own, rows)], plane_all.at[pl.ds(own, rows)], target).start()
        return c

    lax.fori_loop(1, planes, plane_share, 0)
    span_wait(plane_got, recv_sems.at[4])
    back = copy(5, plane_all, out.at[core], partner)
    back.start()
    out[core] = plane_all[...]
    back.wait_recv()
    hop.wait_send()
    span_wait(plane_got, send_sems.at[1])
    span_wait(ring_got, send_sems.at[2])
    span_wait(ring_got, send_sems.at[3])
    span_wait(plane_got, send_sems.at[4])
    back.wait_send()


def sum_scratch(grid, side):
    nx, ny, nz = grid
    planes = nx * ny
    rows = side // planes
    piece = rows // nz
    return [
        pltpu.VMEM((side, side), jnp.bfloat16),
        pltpu.VMEM((side, side), jnp.bfloat16),
        pltpu.VMEM((side, side), jnp.bfloat16),
        pltpu.VMEM((planes - 1, rows, side), jnp.bfloat16),
        pltpu.VMEM((nz, piece, side), jnp.float32),
        pltpu.VMEM((nz - 1, piece, side), jnp.float32),
        pltpu.VMEM((nz, piece, side), jnp.float32),
        pltpu.VMEM((side, side), jnp.bfloat16),
        pltpu.SemaphoreType.DMA((6,)),
        pltpu.SemaphoreType.DMA((6,)),
    ]


def dom_peer(step):
    other = (lax.axis_index("dom") + step) % lax.axis_size("dom")
    return (other, lax.axis_index("rep")), other


def greet_halo_peers(barrier):
    def signal(step, carry):
        pl.semaphore_signal(barrier, inc=1, device_id=dom_peer(step)[0], device_id_type=MESH)
        return carry

    lax.fori_loop(1, lax.axis_size("dom"), signal, 0)


def dot(a, b):
    return jnp.dot(a, b, preferred_element_type=jnp.float32)


def dot_t(a, b):
    return lax.dot_general(a, b, (((0,), (0,)), ((), ())), preferred_element_type=jnp.float32)


def iota(shape, axis):
    return lax.broadcasted_iota(jnp.int32, shape, axis)


def column(row):
    n = row.shape[1]
    picked = jnp.where(iota((n, n), 0) == iota((n, n), 1), jnp.broadcast_to(row, (n, n)), 0)
    return jnp.sum(picked, axis=1, keepdims=True)


def step_kernel(
    grid,
    history,
    tiles_hbm,
    cols,
    send_rows,
    send_count,
    node_ids,
    weights,
    upstream_hbm,
    written,
    total_out,
    hist,
    tiles,
    upstream,
    adj,
    adj_back,
    picker,
    scatter,
    h_start,
    hidden,
    partial,
    mixed,
    slope,
    back,
    send_buf,
    halo_got,
    halo,
    grads,
    local_sems,
    halo_send,
    halo_recv,
    *sum_refs,
):
    nx, ny, nz = grid
    bf16, f32 = jnp.bfloat16, jnp.float32
    batch, width = hist.shape[1], hist.shape[2]
    half = width // 2
    tile = tiles.shape[1]
    blocks, per_row = cols.shape
    batch_blocks = batch // tile
    all_blocks = adj.shape[1] // tile
    owners, cap = send_rows.shape
    chunk = min(256, batch)
    chunks = batch // chunk
    me = lax.axis_index("dom")

    loads = [
        pltpu.make_async_copy(history.at[0], hist.at[0], local_sems.at[0]),
        pltpu.make_async_copy(history.at[1], hist.at[1], local_sems.at[1]),
        pltpu.make_async_copy(tiles_hbm, tiles.at[pl.ds(0, blocks * per_row)], local_sems.at[2]),
        pltpu.make_async_copy(upstream_hbm, upstream, local_sems.at[3]),
    ]
    for load in loads:
        load.start()

    barrier = pltpu.get_barrier_semaphore()
    greet_halo_peers(barrier)
    greet_sum_peers(grid, barrier)

    slots = owners * cap
    slot = iota((slots, 1), 0)
    peer = (me + slot // cap) % owners
    turn = (peer == iota((slots, owners), 1)).astype(f32)
    listed = lax.dot_general(
        turn, send_rows[...].astype(f32), (((1,), (0,)), ((), ())), precision=lax.Precision.HIGHEST, preferred_element_type=f32
    )
    listed = jnp.sum(jnp.where(iota((slots, cap), 1) == slot % cap, listed, 0.0), axis=1, keepdims=True)
    count = jnp.sum(turn * send_count[...].astype(f32), axis=1, keepdims=True)
    wanted = jnp.where((slot % cap).astype(f32) < count, listed, -1.0)
    picker[...] = jnp.where(wanted == iota((slots, batch), 1).astype(f32), 1.0, 0.0).astype(bf16)

    group = max(1, 128 // cap)

    def halo_copy(level, step):
        target, other = dom_peer(step)
        return pltpu.make_async_remote_copy(
            src_ref=send_buf.at[level, step],
            dst_ref=halo_got.at[level, me],
            send_sem=halo_send.at[level],
            recv_sem=halo_recv.at[level],
            device_id=target,
            device_id_type=MESH,
        )

    def fill(level, part):
        start = pl.multiple_of(part * group * cap, group * cap)
        rows = dot(picker[pl.ds(start, group * cap), :], hist[level])
        low = rows[:, :half].reshape(group, cap, half)
        high = rows[:, half:].reshape(group, cap, half)
        send_buf[level, pl.ds(part * group, group)] = jnp.concatenate([low, high], axis=1).astype(bf16)

    def post(level, part):
        def go(step, carry):
            halo_copy(level, step).start()
            return carry

        lax.fori_loop(jnp.maximum(part * group, 1), (part + 1) * group, go, 0)

    for level in range(2):
        loads[level].wait()
        if level == 0:
            fill(0, 0)
            pl.semaphore_wait(barrier, (owners - 1) + 1 + (nx * ny - 1) + (nz - 1))
            post(0, 0)

        def emit(part, carry):
            fill(level, part)
            post(level, part)
            return carry

        lax.fori_loop(1 - level, owners // group, emit, 0)
        halo_got[level, me] = send_buf[level, 0]

    scatter[...] = jnp.where(iota((batch, batch), 0) == node_ids[...], 1.0, 0.0).astype(bf16)
    for part in range(batch // tile):
        ids = column(node_ids[:, part * tile : (part + 1) * tile])
        gather = jnp.where(ids == iota((tile, batch), 1), 1.0, 0.0).astype(bf16)
        h_start[part * tile : (part + 1) * tile] = dot(gather, hist[0]).astype(bf16)

    loads[2].wait()
    tiles[blocks * per_row] = jnp.zeros((tile, tile), bf16)

    def arrange(row, carry):
        down = pl.multiple_of(row * tile, tile)
        for block in range(all_blocks):
            index = blocks * per_row
            for t in range(per_row):
                index = jnp.where(cols[row, t] == block, row * per_row + t, index)
            values = tiles[index]
            adj[pl.ds(down, tile), block * tile : (block + 1) * tile] = values
            if block < batch_blocks:
                adj_back[block * tile : (block + 1) * tile, pl.ds(down, tile)] = values.astype(f32).T.astype(bf16)
        return carry

    lax.fori_loop(0, blocks, arrange, 0)

    def over_chunks(body):
        def run(part, carry):
            body(pl.ds(pl.multiple_of(part * chunk, chunk), chunk))
            return carry

        lax.fori_loop(0, chunks, run, 0)

    def batch_part(source):
        def body(rows):
            partial[rows, :] = dot(adj[rows, :batch], source[...])

        over_chunks(body)

    def receive(level):
        span_wait(send_buf.at[level, pl.ds(0, owners - 1)], halo_recv.at[level])
        got = halo_got[level].astype(f32)
        low = got[:, :cap].reshape(slots, half)
        high = got[:, cap:].reshape(slots, half)
        halo[...] = jnp.concatenate([low, high], axis=1).astype(bf16)

    def preact(level, rows):
        summed = partial[rows, :] + dot(adj[rows, batch:], halo[...])
        mixed_rows = ((1.0 - RESTART) * summed + RESTART * h_start[rows, :].astype(f32)).astype(bf16)
        mixed[level, rows, :] = mixed_rows
        beta = layer_beta(level)
        return (1.0 - beta) * mixed_rows.astype(f32) + beta * dot(mixed_rows, weights[level])

    batch_part(h_start)
    receive(0)

    def first_layer(rows):
        z = preact(0, rows)
        sigma = jax.nn.sigmoid(z)
        hidden[rows, :] = (z * sigma).astype(bf16)
        slope[rows, :] = sigma * (1.0 + z * (1.0 - sigma))

    over_chunks(first_layer)
    batch_part(hidden)

    def write_back(rows):
        written[0, rows, :] = dot(scatter[rows, :], hidden[...]).astype(bf16)

    over_chunks(write_back)
    loads[3].wait()
    receive(1)
    beta_last = layer_beta(1)

    def last_layer(rows):
        z = preact(1, rows)
        grad = (upstream[rows, :].astype(f32) * silu_slope(z)).astype(bf16)
        upstream[rows, :] = grad
        turned = lax.dot_general(grad, weights[1], (((1,), (1,)), ((), ())), preferred_element_type=f32)
        back[rows, :] = ((1.0 - beta_last) * grad.astype(f32) + beta_last * turned).astype(bf16)

    over_chunks(last_layer)
    grads[1] = beta_last * dot_t(mixed[1], upstream[...])

    def first_grad(rows):
        total = dot(adj_back[rows, :], back[...])
        hidden[rows, :] = ((1.0 - RESTART) * total * slope[rows, :]).astype(bf16)

    over_chunks(first_grad)
    grads[0] = layer_beta(0) * dot_t(mixed[0], hidden[...])
    nodes_all = batch * owners * lax.axis_size("rep")
    sum_body(grid, 1.0 / math.sqrt(nodes_all), grads, total_out, *sum_refs)
    for level in range(2):
        span_wait(send_buf.at[level, pl.ds(0, owners - 1)], halo_send.at[level])


def local(grid, history, tile_values, tile_cols, send_rows, send_count, node_ids, weights, upstream):
    levels, batch, width = history.shape
    blocks, per_row, tile, _ = tile_values.shape
    _, owners, cap = send_rows.shape
    slots = owners * cap
    bf16, f32 = jnp.bfloat16, jnp.float32
    vmem = pl.BlockSpec(memory_space=pltpu.VMEM)
    anywhere = pl.BlockSpec(memory_space=pl.ANY)
    written, total = pl.pallas_call(
        functools.partial(step_kernel, grid),
        out_shape=(jax.ShapeDtypeStruct((1, batch, width), bf16), jax.ShapeDtypeStruct((levels, width, width), bf16)),
        in_specs=[anywhere, anywhere, pl.BlockSpec(memory_space=pltpu.SMEM), vmem, vmem, vmem, vmem, anywhere],
        out_specs=(vmem, vmem),
        scratch_shapes=[
            pltpu.VMEM((levels, batch, width), bf16),
            pltpu.VMEM((blocks * per_row + 1, tile, tile), bf16),
            pltpu.VMEM((batch, width), bf16),
            pltpu.VMEM((batch, batch + slots), bf16),
            pltpu.VMEM((batch, batch), bf16),
            pltpu.VMEM((slots, batch), bf16),
            pltpu.VMEM((batch, batch), bf16),
            pltpu.VMEM((batch, width), bf16),
            pltpu.VMEM((batch, width), bf16),
            pltpu.VMEM((batch, width), f32),
            pltpu.VMEM((levels, batch, width), bf16),
            pltpu.VMEM((batch, width), f32),
            pltpu.VMEM((batch, width), bf16),
            pltpu.VMEM((levels, owners, 2 * cap, width // 2), bf16),
            pltpu.VMEM((levels, owners, 2 * cap, width // 2), bf16),
            pltpu.VMEM((slots, width), bf16),
            pltpu.VMEM((levels, width, width), f32),
            pltpu.SemaphoreType.DMA((4,)),
            pltpu.SemaphoreType.DMA((levels,)),
            pltpu.SemaphoreType.DMA((levels,)),
        ]
        + sum_scratch(grid, width),
        compiler_params=pltpu.CompilerParams(collective_id=0, has_side_effects=True, vmem_limit_bytes=56 * 2**20),
    )(
        history,
        tile_values.reshape(blocks * per_row, tile, tile),
        tile_cols,
        send_rows[0],
        send_count,
        node_ids,
        weights,
        upstream,
    )
    return written, total.astype(f32)


def solution(mesh):
    dom, rep = mesh.shape["dom"], mesh.shape["rep"]
    grid = (dom // RING, rep // 2, RING)
    return jax.shard_map(
        functools.partial(local, grid),
        mesh=mesh,
        in_specs=(
            P(None, ("dom", "rep"), None),
            P(("dom", "rep"), None, None, None),
            P(("dom", "rep"), None),
            P(("dom", "rep"), None, None),
            P(("dom", "rep"), None),
            P(("dom", "rep"), None),
            P(),
            P(("dom", "rep"), None),
        ),
        out_specs=(P(None, ("dom", "rep"), None), P()),
        check_vma=False,
    )
```

```python
import functools
import math

import jax
import jax.numpy as jnp
from jax import lax
from jax.experimental import pallas as pl
from jax.experimental.pallas import tpu as pltpu
from jax.sharding import PartitionSpec as P

RESTART = 0.1
RING = 16


def layer_beta(level):
    return math.log(0.5 / (level + 1) + 1.0)


def silu_slope(preact):
    sigma = jax.nn.sigmoid(preact)
    return sigma * (1.0 + preact * (1.0 - sigma))


MESH = pl.DeviceIdType.MESH


def span_wait(ref, sem):
    pltpu.make_async_copy(ref, ref, sem).wait()


def place(grid):
    nx, ny, nz = grid
    dom, rep = lax.axis_index("dom"), lax.axis_index("rep")
    return dom // nz, dom % nz, rep // 2, rep % 2


def far_first(n, turn):
    side = (turn + 1) // 2
    return (n // 2 + side * (1 - 2 * (turn % 2)) + n) % n


def ring_peer(grid, turn):
    nx, ny, nz = grid
    x, z, y, core = place(grid)
    return (x * nz + (z + far_first(nz, turn)) % nz, y * 2 + core)


def halo_peer(grid, turn):
    nx, ny, nz = grid
    x, z, y, core = place(grid)
    return ((x + far_first(nx, turn % nx)) % nx) * nz + (z + far_first(nz, turn // nx)) % nz


def greet(grid, barrier):
    nx, ny, nz = grid
    x, z, y, core = place(grid)
    rep, reps = lax.axis_index("rep"), 2 * ny

    def signal(target):
        pl.semaphore_signal(barrier, inc=1, device_id=target, device_id_type=MESH)

    def halo(turn, carry):
        signal((halo_peer(grid, turn), rep))
        return carry

    def layer(turn, carry):
        signal(((x + turn % nx) % nx * nz + z, (rep + 1 + turn // nx) % reps))
        return carry

    lax.fori_loop(0, nx * nz - 1, halo, 0)
    lax.fori_loop(0, nx * (reps - 1), layer, 0)
    return nx * nz - 1 + nx * (reps - 1)


def link(stage, src, dst, target, send_sems, recv_sems):
    return pltpu.make_async_remote_copy(
        src_ref=src, dst_ref=dst, send_sem=send_sems.at[stage], recv_sem=recv_sems.at[stage], device_id=target, device_id_type=MESH
    )


def layer_share(grid, rows):
    nx, ny, nz = grid
    x, z, y, core = place(grid)
    reps = 2 * ny
    mine = x * reps + y * 2 + core

    def span(index):
        return pl.ds(pl.multiple_of(index * rows, rows), rows)

    def device(index):
        return (index // reps * nz + z, index % reps)

    return mine, span, device


def sum_send(grid, level, source, layer_got, ring_got, send_sems, recv_sems):
    shares, rows = layer_got.shape[0], layer_got.shape[1]
    group = shares // 2
    mine, span, device = layer_share(grid, rows)

    def send(turn, carry):
        index = level * group + (mine + turn) % group
        link(0, source.at[span(index)], layer_got.at[mine], device(index), send_sems, recv_sems).start()
        return carry

    lax.fori_loop(jnp.where(mine // group == level, 1, 0), group, send, 0)


def sum_rest(grid, scale, out, source, layer_got, ring_got, send_sems, recv_sems):
    nx, ny, nz = grid
    shares, rows = layer_got.shape[0], layer_got.shape[1]
    mine, span, device = layer_share(grid, rows)
    z = place(grid)[1]
    layer_got[mine] = source[span(mine), :]
    span_wait(layer_got.at[pl.ds(0, shares - 1)], recv_sems.at[0])
    ring_got[z] = jnp.sum(layer_got[...].astype(jnp.float32), axis=0).astype(jnp.bfloat16)

    def ring_send(turn, carry):
        link(1, ring_got.at[z], ring_got.at[z], ring_peer(grid, turn), send_sems, recv_sems).start()
        return carry

    lax.fori_loop(0, nz - 1, ring_send, 0)
    span_wait(source.at[pl.ds(0, (shares - 1) * rows)], send_sems.at[0])
    span_wait(ring_got.at[pl.ds(0, nz - 1)], recv_sems.at[1])
    total = jnp.sum(ring_got[...].astype(jnp.float32), axis=0) * scale
    source[span(mine), :] = total.astype(jnp.bfloat16)

    def share(turn, carry):
        index = (mine + 1 + (shares // 2 + ny - 1 + turn) % (shares - 1)) % shares
        link(2, source.at[span(mine)], out.at[span(mine)], device(index), send_sems, recv_sems).start()
        return carry

    lax.fori_loop(0, shares - 1, share, 0)
    own = pltpu.make_async_copy(source.at[span(mine)], out.at[span(mine)], send_sems.at[3])
    own.start()
    span_wait(ring_got.at[pl.ds(0, nz - 1)], send_sems.at[1])
    span_wait(source.at[pl.ds(0, (shares - 1) * rows)], send_sems.at[2])
    own.wait()
    span_wait(source.at[pl.ds(0, (shares - 1) * rows)], recv_sems.at[2])


def sum_scratch(grid, levels, side):
    nx, ny, nz = grid
    shares = nx * ny * 2
    rows = levels * side // shares
    return [
        pltpu.VMEM((levels * side, side), jnp.bfloat16),
        pltpu.VMEM((shares, rows, side), jnp.bfloat16),
        pltpu.VMEM((nz, rows, side), jnp.bfloat16),
        pltpu.SemaphoreType.DMA((4,)),
        pltpu.SemaphoreType.DMA((3,)),
    ]


def dot(a, b):
    return jnp.dot(a, b, preferred_element_type=jnp.float32)


def dot_t(a, b):
    return lax.dot_general(a, b, (((0,), (0,)), ((), ())), preferred_element_type=jnp.float32)


def iota(shape, axis):
    return lax.broadcasted_iota(jnp.int32, shape, axis)


def column(row):
    n = row.shape[1]
    picked = jnp.where(iota((n, n), 0) == iota((n, n), 1), jnp.broadcast_to(row, (n, n)), 0)
    return jnp.sum(picked, axis=1, keepdims=True)


def step_kernel(
    grid,
    history,
    tiles_hbm,
    cols_hbm,
    send_rows_hbm,
    send_count_hbm,
    node_ids_hbm,
    weights_hbm,
    upstream_hbm,
    written,
    total_out,
    cols,
    send_rows,
    send_count,
    node_ids,
    weights,
    written_rows,
    hist,
    tiles,
    upstream,
    adj,
    adj_back,
    picker,
    scatter,
    h_start,
    hidden,
    partial,
    mixed,
    slope,
    back,
    send_buf,
    halo_got,
    halo,
    local_sems,
    halo_send,
    halo_recv,
    *sum_refs,
):
    nx, ny, nz = grid
    bf16, f32 = jnp.bfloat16, jnp.float32
    batch, width = hist.shape[1], hist.shape[2]
    half = width // 2
    tile = tiles.shape[1]
    blocks, per_row = cols.shape
    batch_blocks = batch // tile
    all_blocks = adj.shape[1] // tile
    cap, owners = send_rows.shape
    chunk = min(256, batch)
    chunks = batch // chunk
    me = lax.axis_index("dom")

    barrier = pltpu.get_barrier_semaphore()
    loads = [
        pltpu.make_async_copy(src, dst, local_sems.at[place])
        for place, (src, dst) in enumerate(
            [
                (send_rows_hbm, send_rows),
                (send_count_hbm, send_count),
                (history.at[0], hist.at[0]),
                (history.at[1], hist.at[1]),
                (node_ids_hbm, node_ids),
                (cols_hbm, cols),
                (tiles_hbm, tiles.at[pl.ds(0, blocks * per_row)]),
                (weights_hbm, weights),
                (upstream_hbm, upstream),
            ]
        )
    ]
    for load in loads[:3]:
        load.start()
    greeted = greet(grid, barrier)
    for load in loads[3:]:
        load.start()
    for load in loads[:2]:
        load.wait()

    slots = owners * cap
    slot = iota((slots, 1), 0)
    peer = halo_peer(grid, slot // cap)
    turn = (peer == iota((slots, owners), 1)).astype(f32)
    listed = lax.dot_general(
        turn, send_rows[...].astype(f32), (((1,), (1,)), ((), ())), precision=lax.Precision.HIGHEST, preferred_element_type=f32
    )
    listed = jnp.sum(jnp.where(iota((slots, cap), 1) == slot % cap, listed, 0.0), axis=1, keepdims=True)
    count = jnp.sum(turn * send_count[...].astype(f32), axis=1, keepdims=True)
    wanted = jnp.where((slot % cap).astype(f32) < count, listed, -1.0)
    picker[...] = jnp.where(wanted == iota((slots, batch), 1).astype(f32), 1.0, 0.0).astype(bf16)

    group = max(1, 128 // cap)

    def halo_copy(level, turn):
        return pltpu.make_async_remote_copy(
            src_ref=send_buf.at[level, turn],
            dst_ref=halo_got.at[level, me],
            send_sem=halo_send.at[level],
            recv_sem=halo_recv.at[level],
            device_id=(halo_peer(grid, turn), lax.axis_index("rep")),
            device_id_type=MESH,
        )

    def fill(level, part):
        start = pl.multiple_of(part * group * cap, group * cap)
        rows = dot(picker[pl.ds(start, group * cap), :], hist[level])
        low = rows[:, :half].reshape(group, cap, half)
        high = rows[:, half:].reshape(group, cap, half)
        send_buf[level, pl.ds(part * group, group)] = jnp.concatenate([low, high], axis=1).astype(bf16)

    def post(level, part):
        def go(turn, carry):
            halo_copy(level, turn).start()
            return carry

        lax.fori_loop(part * group, jnp.minimum((part + 1) * group, owners - 1), go, 0)

    for level in range(2):
        loads[2 + level].wait()
        if level == 0:
            fill(0, 0)
            pl.semaphore_wait(barrier, greeted)
            post(0, 0)

        def emit(part, carry):
            fill(level, part)
            post(level, part)
            return carry

        lax.fori_loop(1 - level, owners // group, emit, 0)
        halo_got[level, me] = send_buf[level, owners - 1]

    loads[4].wait()
    scatter[...] = jnp.where(iota((batch, batch), 0) == node_ids[...], 1.0, 0.0).astype(bf16)
    for part in range(batch // tile):
        ids = column(node_ids[:, part * tile : (part + 1) * tile])
        gather = jnp.where(ids == iota((tile, batch), 1), 1.0, 0.0).astype(bf16)
        h_start[part * tile : (part + 1) * tile] = dot(gather, hist[0]).astype(bf16)

    loads[5].wait()
    loads[6].wait()
    tiles[blocks * per_row] = jnp.zeros((tile, tile), bf16)

    def arrange(row, carry):
        down = pl.multiple_of(row * tile, tile)
        for block in range(all_blocks):
            index = blocks * per_row
            for t in range(per_row):
                index = jnp.where(cols[row, t] == block, row * per_row + t, index)
            values = tiles[index]
            adj[pl.ds(down, tile), block * tile : (block + 1) * tile] = values
            if block < batch_blocks:
                adj_back[block * tile : (block + 1) * tile, pl.ds(down, tile)] = values.astype(f32).T.astype(bf16)
        return carry

    lax.fori_loop(0, blocks, arrange, 0)

    def over_chunks(body):
        def run(part, carry):
            body(pl.ds(pl.multiple_of(part * chunk, chunk), chunk))
            return carry

        lax.fori_loop(0, chunks, run, 0)

    def batch_part(source):
        def body(rows):
            partial[rows, :] = dot(adj[rows, :batch], source[...])

        over_chunks(body)

    def receive(level):
        span_wait(send_buf.at[level, pl.ds(0, owners - 1)], halo_recv.at[level])
        got = halo_got[level].astype(f32)
        low = got[:, :cap].reshape(slots, half)
        high = got[:, cap:].reshape(slots, half)
        halo[...] = jnp.concatenate([low, high], axis=1).astype(bf16)

    def preact(level, rows):
        summed = partial[rows, :] + dot(adj[rows, batch:], halo[...])
        mixed_rows = ((1.0 - RESTART) * summed + RESTART * h_start[rows, :].astype(f32)).astype(bf16)
        mixed[level, rows, :] = mixed_rows
        beta = layer_beta(level)
        return (1.0 - beta) * mixed_rows.astype(f32) + beta * dot(mixed_rows, weights[level])

    batch_part(h_start)
    loads[7].wait()
    receive(0)

    def first_layer(rows):
        z = preact(0, rows)
        sigma = jax.nn.sigmoid(z)
        hidden[rows, :] = (z * sigma).astype(bf16)
        slope[rows, :] = sigma * (1.0 + z * (1.0 - sigma))

    over_chunks(first_layer)
    batch_part(hidden)

    def write_back(rows):
        written_rows[rows, :] = dot(scatter[rows, :], hidden[...]).astype(bf16)

    over_chunks(write_back)
    store = pltpu.make_async_copy(written_rows, written.at[0], local_sems.at[len(loads)])
    store.start()
    loads[8].wait()
    receive(1)
    beta_last = layer_beta(1)

    def last_layer(rows):
        z = preact(1, rows)
        grad = (upstream[rows, :].astype(f32) * silu_slope(z)).astype(bf16)
        upstream[rows, :] = grad
        turned = lax.dot_general(grad, weights[1], (((1,), (1,)), ((), ())), preferred_element_type=f32)
        back[rows, :] = ((1.0 - beta_last) * grad.astype(f32) + beta_last * turned).astype(bf16)

    over_chunks(last_layer)
    source = sum_refs[0]
    source[width:, :] = (beta_last * dot_t(mixed[1], upstream[...])).astype(bf16)
    sum_send(grid, 1, *sum_refs)

    def first_grad(rows):
        total = dot(adj_back[rows, :], back[...])
        hidden[rows, :] = ((1.0 - RESTART) * total * slope[rows, :]).astype(bf16)

    over_chunks(first_grad)
    source[:width, :] = (layer_beta(0) * dot_t(mixed[0], hidden[...])).astype(bf16)
    sum_send(grid, 0, *sum_refs)
    nodes_all = batch * owners * lax.axis_size("rep")
    sum_rest(grid, 1.0 / math.sqrt(nodes_all), total_out, *sum_refs)
    store.wait()
    for level in range(2):
        span_wait(send_buf.at[level, pl.ds(0, owners - 1)], halo_send.at[level])


def local(grid, history, tile_values, tile_cols, send_rows, send_count, node_ids, weights, upstream):
    levels, batch, width = history.shape
    blocks, per_row, tile, _ = tile_values.shape
    _, owners, cap = send_rows.shape
    slots = owners * cap
    bf16, f32 = jnp.bfloat16, jnp.float32
    vmem = pl.BlockSpec(memory_space=pltpu.VMEM)
    anywhere = pl.BlockSpec(memory_space=pl.ANY)
    written, total = pl.pallas_call(
        functools.partial(step_kernel, grid),
        out_shape=(jax.ShapeDtypeStruct((1, batch, width), bf16), jax.ShapeDtypeStruct((levels * width, width), bf16)),
        in_specs=[anywhere] * 8,
        out_specs=(anywhere, anywhere),
        scratch_shapes=[
            pltpu.SMEM((blocks, per_row), jnp.int32),
            pltpu.VMEM((cap, owners), jnp.int32),
            pltpu.VMEM((1, owners), jnp.int32),
            pltpu.VMEM((1, batch), jnp.int32),
            pltpu.VMEM((levels, width, width), bf16),
            pltpu.VMEM((batch, width), bf16),
            pltpu.VMEM((levels, batch, width), bf16),
            pltpu.VMEM((blocks * per_row + 1, tile, tile), bf16),
            pltpu.VMEM((batch, width), bf16),
            pltpu.VMEM((batch, batch + slots), bf16),
            pltpu.VMEM((batch, batch), bf16),
            pltpu.VMEM((slots, batch), bf16),
            pltpu.VMEM((batch, batch), bf16),
            pltpu.VMEM((batch, width), bf16),
            pltpu.VMEM((batch, width), bf16),
            pltpu.VMEM((batch, width), f32),
            pltpu.VMEM((levels, batch, width), bf16),
            pltpu.VMEM((batch, width), f32),
            pltpu.VMEM((batch, width), bf16),
            pltpu.VMEM((levels, owners, 2 * cap, width // 2), bf16),
            pltpu.VMEM((levels, owners, 2 * cap, width // 2), bf16),
            pltpu.VMEM((slots, width), bf16),
            pltpu.SemaphoreType.DMA((10,)),
            pltpu.SemaphoreType.DMA((levels,)),
            pltpu.SemaphoreType.DMA((levels,)),
        ]
        + sum_scratch(grid, levels, width),
        compiler_params=pltpu.CompilerParams(collective_id=0, has_side_effects=True, vmem_limit_bytes=56 * 2**20),
    )(
        history,
        tile_values.reshape(blocks * per_row, tile, tile),
        tile_cols,
        send_rows[0].T,
        send_count,
        node_ids,
        weights,
        upstream,
    )

    def finish(written_ref, total_ref, written_out, total_out):
        written_out[...] = written_ref[...]
        for level in range(levels):
            total_out[level] = total_ref[level * width : (level + 1) * width].astype(f32)

    return pl.pallas_call(
        finish,
        out_shape=(jax.ShapeDtypeStruct(written.shape, bf16), jax.ShapeDtypeStruct((levels, width, width), f32)),
        in_specs=[vmem, vmem],
        out_specs=(vmem, vmem),
    )(written, total)


def solution(mesh):
    dom, rep = mesh.shape["dom"], mesh.shape["rep"]
    grid = (dom // RING, rep // 2, RING)
    return jax.shard_map(
        functools.partial(local, grid),
        mesh=mesh,
        in_specs=(
            P(None, ("dom", "rep"), None),
            P(("dom", "rep"), None, None, None),
            P(("dom", "rep"), None),
            P(("dom", "rep"), None, None),
            P(("dom", "rep"), None),
            P(("dom", "rep"), None),
            P(),
            P(("dom", "rep"), None),
        ),
        out_specs=(P(None, ("dom", "rep"), None), P()),
        check_vma=False,
    )
```

```python
import functools
import math

import jax
import jax.numpy as jnp
from jax import lax
from jax.experimental import pallas as pl
from jax.experimental.pallas import tpu as pltpu
from jax.sharding import PartitionSpec as P

RESTART = 0.1
RING = 16


def layer_beta(level):
    return math.log(0.5 / (level + 1) + 1.0)


def silu_slope(preact):
    sigma = jax.nn.sigmoid(preact)
    return sigma * (1.0 + preact * (1.0 - sigma))


MESH = pl.DeviceIdType.MESH


def span_wait(ref, sem):
    pltpu.make_async_copy(ref, ref, sem).wait()


def place(grid):
    nx, ny, nz = grid
    dom, rep = lax.axis_index("dom"), lax.axis_index("rep")
    return dom // nz, dom % nz, rep // 2, rep % 2


def far_first(n, turn):
    side = (turn + 1) // 2
    return (n // 2 + side * (1 - 2 * (turn % 2)) + n) % n


def ring_peer(grid, turn):
    nx, ny, nz = grid
    x, z, y, core = place(grid)
    return (x * nz + (z + far_first(nz, turn)) % nz, y * 2 + core)


def halo_peer(grid, turn):
    nx, ny, nz = grid
    x, z, y, core = place(grid)
    return ((x + far_first(nx, turn % nx)) % nx) * nz + (z + far_first(nz, turn // nx)) % nz


def greet(grid, barrier):
    nx, ny, nz = grid
    x, z, y, core = place(grid)
    rep, reps = lax.axis_index("rep"), 2 * ny

    def signal(target):
        pl.semaphore_signal(barrier, inc=1, device_id=target, device_id_type=MESH)

    def halo(turn, carry):
        signal((halo_peer(grid, turn), rep))
        return carry

    def layer(turn, carry):
        signal(((x + turn % nx) % nx * nz + z, (rep + 1 + turn // nx) % reps))
        return carry

    far = nx * nz // 2
    lax.fori_loop(0, far, halo, 0)
    lax.fori_loop(0, nx * (reps - 1), layer, 0)
    lax.fori_loop(far, nx * nz - 1, halo, 0)
    return nx * nz - 1 + nx * (reps - 1)


def link(stage, src, dst, target, send_sems, recv_sems):
    return pltpu.make_async_remote_copy(
        src_ref=src, dst_ref=dst, send_sem=send_sems.at[stage], recv_sem=recv_sems.at[stage], device_id=target, device_id_type=MESH
    )


def layer_share(grid, rows):
    nx, ny, nz = grid
    x, z, y, core = place(grid)
    reps = 2 * ny
    mine = x * reps + y * 2 + core

    def span(index):
        return pl.ds(pl.multiple_of(index * rows, rows), rows)

    def device(index):
        return (index // reps * nz + z, index % reps)

    return mine, span, device


def sum_send(grid, level, source, layer_got, ring_got, send_sems, recv_sems):
    shares, rows = layer_got.shape[0], layer_got.shape[1]
    group = shares // 2
    mine, span, device = layer_share(grid, rows)

    def send(turn, carry):
        index = level * group + (mine + turn) % group
        link(0, source.at[span(index)], layer_got.at[mine], device(index), send_sems, recv_sems).start()
        return carry

    lax.fori_loop(jnp.where(mine // group == level, 1, 0), group, send, 0)


def sum_rest(grid, scale, out, source, layer_got, ring_got, send_sems, recv_sems):
    nx, ny, nz = grid
    shares, rows = layer_got.shape[0], layer_got.shape[1]
    mine, span, device = layer_share(grid, rows)
    z = place(grid)[1]
    layer_got[mine] = source[span(mine), :]
    span_wait(layer_got.at[pl.ds(0, shares - 1)], recv_sems.at[0])
    ring_got[z] = jnp.sum(layer_got[...].astype(jnp.float32), axis=0).astype(jnp.bfloat16)

    def ring_send(turn, carry):
        link(1, ring_got.at[z], ring_got.at[z], ring_peer(grid, turn), send_sems, recv_sems).start()
        return carry

    lax.fori_loop(0, nz - 1, ring_send, 0)
    span_wait(source.at[pl.ds(0, (shares - 1) * rows)], send_sems.at[0])
    span_wait(ring_got.at[pl.ds(0, nz - 1)], recv_sems.at[1])
    total = jnp.sum(ring_got[...].astype(jnp.float32), axis=0) * scale
    source[span(mine), :] = total.astype(jnp.bfloat16)

    def share(turn, carry):
        index = (mine + 1 + (shares // 2 + ny - 1 + turn) % (shares - 1)) % shares
        link(2, source.at[span(mine)], out.at[span(mine)], device(index), send_sems, recv_sems).start()
        return carry

    lax.fori_loop(0, shares - 1, share, 0)
    own = pltpu.make_async_copy(source.at[span(mine)], out.at[span(mine)], send_sems.at[3])
    own.start()
    span_wait(ring_got.at[pl.ds(0, nz - 1)], send_sems.at[1])
    span_wait(source.at[pl.ds(0, (shares - 1) * rows)], send_sems.at[2])
    own.wait()
    span_wait(source.at[pl.ds(0, (shares - 1) * rows)], recv_sems.at[2])


def sum_scratch(grid, levels, side):
    nx, ny, nz = grid
    shares = nx * ny * 2
    rows = levels * side // shares
    return [
        pltpu.VMEM((levels * side, side), jnp.bfloat16),
        pltpu.VMEM((shares, rows, side), jnp.bfloat16),
        pltpu.VMEM((nz, rows, side), jnp.bfloat16),
        pltpu.SemaphoreType.DMA((4,)),
        pltpu.SemaphoreType.DMA((3,)),
    ]


def dot(a, b):
    return jnp.dot(a, b, preferred_element_type=jnp.float32)


def dot_t(a, b):
    return lax.dot_general(a, b, (((0,), (0,)), ((), ())), preferred_element_type=jnp.float32)


def iota(shape, axis):
    return lax.broadcasted_iota(jnp.int32, shape, axis)


def column(row):
    n = row.shape[1]
    picked = jnp.where(iota((n, n), 0) == iota((n, n), 1), jnp.broadcast_to(row, (n, n)), 0)
    return jnp.sum(picked, axis=1, keepdims=True)


def step_kernel(
    grid,
    history,
    tiles_hbm,
    cols_hbm,
    send_rows_hbm,
    send_count_hbm,
    node_ids_hbm,
    weights_hbm,
    upstream_hbm,
    written,
    total_out,
    cols,
    send_rows,
    send_count,
    node_ids,
    weights,
    written_rows,
    hist,
    tiles,
    upstream,
    adj,
    adj_back,
    picker,
    scatter,
    h_start,
    hidden,
    partial,
    mixed,
    slope,
    back,
    send_buf,
    halo_got,
    halo,
    local_sems,
    halo_send,
    halo_recv,
    *sum_refs,
):
    nx, ny, nz = grid
    bf16, f32 = jnp.bfloat16, jnp.float32
    batch, width = hist.shape[1], hist.shape[2]
    half = width // 2
    tile = tiles.shape[1]
    blocks, per_row = cols.shape
    batch_blocks = batch // tile
    all_blocks = adj.shape[1] // tile
    cap, owners = send_rows.shape
    chunk = min(512, batch)
    chunks = batch // chunk
    me = lax.axis_index("dom")

    barrier = pltpu.get_barrier_semaphore()
    loads = [
        pltpu.make_async_copy(src, dst, local_sems.at[order])
        for order, (src, dst) in enumerate(
            [
                (send_rows_hbm, send_rows),
                (send_count_hbm, send_count),
                (history.at[0], hist.at[0]),
                (history.at[1], hist.at[1]),
                (node_ids_hbm, node_ids),
                (cols_hbm, cols),
                (tiles_hbm, tiles.at[pl.ds(0, blocks * per_row)]),
                (weights_hbm, weights),
                (upstream_hbm, upstream),
            ]
        )
    ]
    for load in loads[:3]:
        load.start()
    greeted = greet(grid, barrier)
    for load in loads[3:]:
        load.start()
    for load in loads[:2]:
        load.wait()

    slots = owners * cap
    slot = iota((slots, 1), 0)
    peer = halo_peer(grid, slot // cap)
    turn = (peer == iota((slots, owners), 1)).astype(f32)
    listed = lax.dot_general(
        turn, send_rows[...].astype(f32), (((1,), (1,)), ((), ())), precision=lax.Precision.HIGHEST, preferred_element_type=f32
    )
    listed = jnp.sum(jnp.where(iota((slots, cap), 1) == slot % cap, listed, 0.0), axis=1, keepdims=True)
    count = jnp.sum(turn * send_count[...].astype(f32), axis=1, keepdims=True)
    wanted = jnp.where((slot % cap).astype(f32) < count, listed, -1.0)
    picker[...] = jnp.where(wanted == iota((slots, batch), 1).astype(f32), 1.0, 0.0).astype(bf16)

    group = max(1, 128 // cap)

    def halo_copy(level, turn):
        return pltpu.make_async_remote_copy(
            src_ref=send_buf.at[level, turn],
            dst_ref=halo_got.at[level, me],
            send_sem=halo_send.at[level],
            recv_sem=halo_recv.at[level],
            device_id=(halo_peer(grid, turn), lax.axis_index("rep")),
            device_id_type=MESH,
        )

    def fill(level, part):
        start = pl.multiple_of(part * group * cap, group * cap)
        rows = dot(picker[pl.ds(start, group * cap), :], hist[level])
        low = rows[:, :half].reshape(group, cap, half)
        high = rows[:, half:].reshape(group, cap, half)
        send_buf[level, pl.ds(part * group, group)] = jnp.concatenate([low, high], axis=1).astype(bf16)

    def post(level, part):
        def go(turn, carry):
            halo_copy(level, turn).start()
            return carry

        lax.fori_loop(part * group, jnp.minimum((part + 1) * group, owners - 1), go, 0)

    for level in range(2):
        loads[2 + level].wait()
        if level == 0:
            fill(0, 0)
            pl.semaphore_wait(barrier, greeted)
            post(0, 0)

        def emit(part, carry):
            fill(level, part)
            post(level, part)
            return carry

        lax.fori_loop(1 - level, owners // group, emit, 0)
        halo_got[level, me] = send_buf[level, owners - 1]

    loads[4].wait()
    scatter[...] = jnp.where(iota((batch, batch), 0) == node_ids[...], 1.0, 0.0).astype(bf16)
    for part in range(batch // tile):
        ids = column(node_ids[:, part * tile : (part + 1) * tile])
        gather = jnp.where(ids == iota((tile, batch), 1), 1.0, 0.0).astype(bf16)
        h_start[part * tile : (part + 1) * tile] = dot(gather, hist[0]).astype(bf16)

    loads[5].wait()
    loads[6].wait()
    tiles[blocks * per_row] = jnp.zeros((tile, tile), bf16)

    def arrange(row, carry):
        down = pl.multiple_of(row * tile, tile)
        for block in range(all_blocks):
            index = blocks * per_row
            for t in range(per_row):
                index = jnp.where(cols[row, t] == block, row * per_row + t, index)
            values = tiles[index]
            adj[pl.ds(down, tile), block * tile : (block + 1) * tile] = values
            if block < batch_blocks:
                adj_back[block * tile : (block + 1) * tile, pl.ds(down, tile)] = values.astype(f32).T.astype(bf16)
        return carry

    lax.fori_loop(0, blocks, arrange, 0)

    def over_chunks(body):
        for part in range(chunks):
            body(pl.ds(part * chunk, chunk))

    def batch_part(source):
        def body(rows):
            partial[rows, :] = dot(adj[rows, :batch], source[...])

        over_chunks(body)

    def receive(level):
        span_wait(send_buf.at[level, pl.ds(0, owners - 1)], halo_recv.at[level])
        got = halo_got[level].astype(f32)
        low = got[:, :cap].reshape(slots, half)
        high = got[:, cap:].reshape(slots, half)
        halo[...] = jnp.concatenate([low, high], axis=1).astype(bf16)

    def preact(level, rows):
        summed = partial[rows, :] + dot(adj[rows, batch:], halo[...])
        mixed_rows = ((1.0 - RESTART) * summed + RESTART * h_start[rows, :].astype(f32)).astype(bf16)
        mixed[level, rows, :] = mixed_rows
        beta = layer_beta(level)
        return (1.0 - beta) * mixed_rows.astype(f32) + beta * dot(mixed_rows, weights[level])

    batch_part(h_start)
    loads[7].wait()
    receive(0)

    def first_layer(rows):
        z = preact(0, rows)
        sigma = jax.nn.sigmoid(z)
        hidden[rows, :] = (z * sigma).astype(bf16)
        slope[rows, :] = sigma * (1.0 + z * (1.0 - sigma))

    over_chunks(first_layer)
    batch_part(hidden)

    def write_back(rows):
        written_rows[rows, :] = dot(scatter[rows, :], hidden[...]).astype(bf16)

    over_chunks(write_back)
    store = pltpu.make_async_copy(written_rows, written.at[0], local_sems.at[len(loads)])
    store.start()
    loads[8].wait()
    receive(1)
    beta_last = layer_beta(1)

    def last_layer(rows):
        z = preact(1, rows)
        grad = (upstream[rows, :].astype(f32) * silu_slope(z)).astype(bf16)
        upstream[rows, :] = grad
        turned = lax.dot_general(grad, weights[1], (((1,), (1,)), ((), ())), preferred_element_type=f32)
        back[rows, :] = ((1.0 - beta_last) * grad.astype(f32) + beta_last * turned).astype(bf16)

    over_chunks(last_layer)
    source = sum_refs[0]
    source[width:, :] = (beta_last * dot_t(mixed[1], upstream[...])).astype(bf16)
    sum_send(grid, 1, *sum_refs)

    def first_grad(rows):
        total = dot(adj_back[rows, :], back[...])
        hidden[rows, :] = ((1.0 - RESTART) * total * slope[rows, :]).astype(bf16)

    over_chunks(first_grad)
    source[:width, :] = (layer_beta(0) * dot_t(mixed[0], hidden[...])).astype(bf16)
    sum_send(grid, 0, *sum_refs)
    nodes_all = batch * owners * lax.axis_size("rep")
    sum_rest(grid, 1.0 / math.sqrt(nodes_all), total_out, *sum_refs)
    store.wait()
    for level in range(2):
        span_wait(send_buf.at[level, pl.ds(0, owners - 1)], halo_send.at[level])


def local(grid, history, tile_values, tile_cols, send_rows, send_count, node_ids, weights, upstream):
    levels, batch, width = history.shape
    blocks, per_row, tile, _ = tile_values.shape
    _, owners, cap = send_rows.shape
    slots = owners * cap
    bf16, f32 = jnp.bfloat16, jnp.float32
    vmem = pl.BlockSpec(memory_space=pltpu.VMEM)
    anywhere = pl.BlockSpec(memory_space=pl.ANY)
    written, total = pl.pallas_call(
        functools.partial(step_kernel, grid),
        out_shape=(jax.ShapeDtypeStruct((1, batch, width), bf16), jax.ShapeDtypeStruct((levels * width, width), bf16)),
        in_specs=[anywhere] * 8,
        out_specs=(anywhere, anywhere),
        scratch_shapes=[
            pltpu.SMEM((blocks, per_row), jnp.int32),
            pltpu.VMEM((cap, owners), jnp.int32),
            pltpu.VMEM((1, owners), jnp.int32),
            pltpu.VMEM((1, batch), jnp.int32),
            pltpu.VMEM((levels, width, width), bf16),
            pltpu.VMEM((batch, width), bf16),
            pltpu.VMEM((levels, batch, width), bf16),
            pltpu.VMEM((blocks * per_row + 1, tile, tile), bf16),
            pltpu.VMEM((batch, width), bf16),
            pltpu.VMEM((batch, batch + slots), bf16),
            pltpu.VMEM((batch, batch), bf16),
            pltpu.VMEM((slots, batch), bf16),
            pltpu.VMEM((batch, batch), bf16),
            pltpu.VMEM((batch, width), bf16),
            pltpu.VMEM((batch, width), bf16),
            pltpu.VMEM((batch, width), f32),
            pltpu.VMEM((levels, batch, width), bf16),
            pltpu.VMEM((batch, width), f32),
            pltpu.VMEM((batch, width), bf16),
            pltpu.VMEM((levels, owners, 2 * cap, width // 2), bf16),
            pltpu.VMEM((levels, owners, 2 * cap, width // 2), bf16),
            pltpu.VMEM((slots, width), bf16),
            pltpu.SemaphoreType.DMA((10,)),
            pltpu.SemaphoreType.DMA((levels,)),
            pltpu.SemaphoreType.DMA((levels,)),
        ]
        + sum_scratch(grid, levels, width),
        compiler_params=pltpu.CompilerParams(collective_id=0, has_side_effects=True, vmem_limit_bytes=56 * 2**20),
    )(
        history,
        tile_values.reshape(blocks * per_row, tile, tile),
        tile_cols,
        send_rows[0].T,
        send_count,
        node_ids,
        weights,
        upstream,
    )

    def finish(written_ref, total_ref, written_out, total_out):
        written_out[...] = written_ref[...]
        for level in range(levels):
            total_out[level] = total_ref[level * width : (level + 1) * width].astype(f32)

    return pl.pallas_call(
        finish,
        out_shape=(jax.ShapeDtypeStruct(written.shape, bf16), jax.ShapeDtypeStruct((levels, width, width), f32)),
        in_specs=[vmem, vmem],
        out_specs=(vmem, vmem),
    )(written, total)


def solution(mesh):
    dom, rep = mesh.shape["dom"], mesh.shape["rep"]
    grid = (dom // RING, rep // 2, RING)
    return jax.shard_map(
        functools.partial(local, grid),
        mesh=mesh,
        in_specs=(
            P(None, ("dom", "rep"), None),
            P(("dom", "rep"), None, None, None),
            P(("dom", "rep"), None),
            P(("dom", "rep"), None, None),
            P(("dom", "rep"), None),
            P(("dom", "rep"), None),
            P(),
            P(("dom", "rep"), None),
        ),
        out_specs=(P(None, ("dom", "rep"), None), P()),
        check_vma=False,
    )
```

```python
import functools
import math

import jax
import jax.numpy as jnp
from jax import lax
from jax.experimental import pallas as pl
from jax.experimental.pallas import tpu as pltpu
from jax.sharding import PartitionSpec as P

RESTART = 0.1
RING = 16


def layer_beta(level):
    return math.log(0.5 / (level + 1) + 1.0)


def silu_slope(preact):
    sigma = jax.nn.sigmoid(preact)
    return sigma * (1.0 + preact * (1.0 - sigma))


MESH = pl.DeviceIdType.MESH


def span_wait(ref, sem):
    pltpu.make_async_copy(ref, ref, sem).wait()


def place(grid):
    nx, ny, nz = grid
    dom, rep = lax.axis_index("dom"), lax.axis_index("rep")
    return dom // nz, dom % nz, rep // 2, rep % 2


def far_first(n, turn):
    side = (turn + 1) // 2
    return (n // 2 + side * (1 - 2 * (turn % 2)) + n) % n


def ring_peer(grid, turn):
    nx, ny, nz = grid
    x, z, y, core = place(grid)
    return (x * nz + (z + far_first(nz, turn)) % nz, y * 2 + core)


def halo_peer(grid, turn):
    nx, ny, nz = grid
    x, z, y, core = place(grid)
    return ((x + far_first(nx, turn % nx)) % nx) * nz + (z + far_first(nz, turn // nx)) % nz


def greet(grid, barrier):
    nx, ny, nz = grid
    x, z, y, core = place(grid)
    rep, reps = lax.axis_index("rep"), 2 * ny

    def signal(target):
        pl.semaphore_signal(barrier, inc=1, device_id=target, device_id_type=MESH)

    def halo(turn, carry):
        signal((halo_peer(grid, turn), rep))
        return carry

    def layer(turn, carry):
        signal(((x + turn % nx) % nx * nz + z, (rep + 1 + turn // nx) % reps))
        return carry

    far = nx * nz // 2
    lax.fori_loop(0, far, halo, 0)
    lax.fori_loop(0, nx * (reps - 1), layer, 0)
    lax.fori_loop(far, nx * nz - 1, halo, 0)
    return nx * nz - 1 + nx * (reps - 1)


def link(stage, src, dst, target, send_sems, recv_sems):
    return pltpu.make_async_remote_copy(
        src_ref=src, dst_ref=dst, send_sem=send_sems.at[stage], recv_sem=recv_sems.at[stage], device_id=target, device_id_type=MESH
    )


def layer_share(grid, rows):
    nx, ny, nz = grid
    x, z, y, core = place(grid)
    reps = 2 * ny
    mine = x * reps + y * 2 + core

    def span(index):
        return pl.ds(pl.multiple_of(index * rows, rows), rows)

    def device(index):
        return (index // reps * nz + z, index % reps)

    return mine, span, device


def sum_send(grid, level, source, layer_got, ring_got, send_sems, recv_sems):
    shares, rows = layer_got.shape[0], layer_got.shape[1]
    group = shares // 2
    mine, span, device = layer_share(grid, rows)

    same = jnp.where(mine // group == level, 1, 0)

    def send(turn, carry):
        step = turn + 3
        step = jnp.where(step >= group - same, step - (group - same), step)
        index = level * group + (mine + same + step) % group
        link(0, source.at[span(index)], layer_got.at[mine], device(index), send_sems, recv_sems).start()
        return carry

    lax.fori_loop(0, group - same, send, 0)


def sum_rest(grid, scale, out, source, layer_got, ring_got, send_sems, recv_sems):
    nx, ny, nz = grid
    shares, rows = layer_got.shape[0], layer_got.shape[1]
    mine, span, device = layer_share(grid, rows)
    z = place(grid)[1]
    layer_got[mine] = source[span(mine), :]
    span_wait(layer_got.at[pl.ds(0, shares - 1)], recv_sems.at[0])
    ring_got[z] = jnp.sum(layer_got[...].astype(jnp.float32), axis=0).astype(jnp.bfloat16)

    def ring_send(turn, carry):
        link(1, ring_got.at[z], ring_got.at[z], ring_peer(grid, turn), send_sems, recv_sems).start()
        return carry

    lax.fori_loop(0, nz - 1, ring_send, 0, unroll=nz - 1)
    span_wait(source.at[pl.ds(0, (shares - 1) * rows)], send_sems.at[0])
    span_wait(ring_got.at[pl.ds(0, nz - 1)], recv_sems.at[1])
    total = jnp.sum(ring_got[...].astype(jnp.float32), axis=0) * scale
    source[span(mine), :] = total.astype(jnp.bfloat16)

    def share(turn, carry):
        index = (mine + 1 + (shares // 2 + ny - 1 + turn) % (shares - 1)) % shares
        link(2, source.at[span(mine)], out.at[span(mine)], device(index), send_sems, recv_sems).start()
        return carry

    lax.fori_loop(0, shares - 1, share, 0, unroll=shares - 1)
    own = pltpu.make_async_copy(source.at[span(mine)], out.at[span(mine)], send_sems.at[3])
    own.start()
    span_wait(ring_got.at[pl.ds(0, nz - 1)], send_sems.at[1])
    span_wait(source.at[pl.ds(0, (shares - 1) * rows)], send_sems.at[2])
    own.wait()
    span_wait(source.at[pl.ds(0, (shares - 1) * rows)], recv_sems.at[2])


def sum_scratch(grid, levels, side):
    nx, ny, nz = grid
    shares = nx * ny * 2
    rows = levels * side // shares
    return [
        pltpu.VMEM((levels * side, side), jnp.bfloat16),
        pltpu.VMEM((shares, rows, side), jnp.bfloat16),
        pltpu.VMEM((nz, rows, side), jnp.bfloat16),
        pltpu.SemaphoreType.DMA((4,)),
        pltpu.SemaphoreType.DMA((3,)),
    ]


def dot(a, b):
    return jnp.dot(a, b, preferred_element_type=jnp.float32)


def dot_t(a, b):
    return lax.dot_general(a, b, (((0,), (0,)), ((), ())), preferred_element_type=jnp.float32)


def iota(shape, axis):
    return lax.broadcasted_iota(jnp.int32, shape, axis)


def column(row):
    n = row.shape[1]
    picked = jnp.where(iota((n, n), 0) == iota((n, n), 1), jnp.broadcast_to(row, (n, n)), 0)
    return jnp.sum(picked, axis=1, keepdims=True)


def step_kernel(
    grid,
    history,
    tiles_hbm,
    cols_hbm,
    send_rows_hbm,
    send_count_hbm,
    node_ids_hbm,
    weights_hbm,
    upstream_hbm,
    written,
    total_out,
    cols,
    send_rows,
    send_count,
    node_ids,
    weights,
    written_rows,
    hist,
    tiles,
    upstream,
    adj,
    adj_back,
    picker,
    scatter,
    h_start,
    hidden,
    partial,
    mixed,
    slope,
    back,
    mixed_turned,
    weight_turned,
    send_buf,
    halo_got,
    halo,
    local_sems,
    halo_send,
    halo_recv,
    *sum_refs,
):
    nx, ny, nz = grid
    bf16, f32 = jnp.bfloat16, jnp.float32
    batch, width = hist.shape[1], hist.shape[2]
    half = width // 2
    tile = tiles.shape[1]
    blocks, per_row = cols.shape
    batch_blocks = batch // tile
    all_blocks = adj.shape[1] // tile
    cap, owners = send_rows.shape
    chunk = min(512, batch)
    chunks = batch // chunk
    me = lax.axis_index("dom")

    barrier = pltpu.get_barrier_semaphore()
    loads = [
        pltpu.make_async_copy(src, dst, local_sems.at[order])
        for order, (src, dst) in enumerate(
            [
                (send_rows_hbm, send_rows),
                (send_count_hbm, send_count),
                (history.at[0], hist.at[0]),
                (history.at[1], hist.at[1]),
                (node_ids_hbm, node_ids),
                (cols_hbm, cols),
                (tiles_hbm, tiles.at[pl.ds(0, blocks * per_row)]),
                (weights_hbm, weights),
                (upstream_hbm, upstream),
            ]
        )
    ]
    for load in loads[:3]:
        load.start()
    greeted = greet(grid, barrier)
    for load in loads[3:]:
        load.start()
    for load in loads[:2]:
        load.wait()

    slots = owners * cap
    slot = iota((slots, 1), 0)
    peer = halo_peer(grid, slot // cap)
    turn = (peer == iota((slots, owners), 1)).astype(f32)
    listed = lax.dot_general(
        turn, send_rows[...].astype(f32), (((1,), (1,)), ((), ())), precision=lax.Precision.HIGHEST, preferred_element_type=f32
    )
    listed = jnp.sum(jnp.where(iota((slots, cap), 1) == slot % cap, listed, 0.0), axis=1, keepdims=True)
    count = jnp.sum(turn * send_count[...].astype(f32), axis=1, keepdims=True)
    wanted = jnp.where((slot % cap).astype(f32) < count, listed, -1.0)
    picker[...] = jnp.where(wanted == iota((slots, batch), 1).astype(f32), 1.0, 0.0).astype(bf16)

    group = max(1, 128 // cap)

    def halo_copy(level, turn):
        return pltpu.make_async_remote_copy(
            src_ref=send_buf.at[level, turn],
            dst_ref=halo_got.at[level, me],
            send_sem=halo_send.at[level],
            recv_sem=halo_recv.at[level],
            device_id=(halo_peer(grid, turn), lax.axis_index("rep")),
            device_id_type=MESH,
        )

    def fill(level, part):
        start = pl.multiple_of(part * group * cap, group * cap)
        rows = dot(picker[pl.ds(start, group * cap), :], hist[level])
        low = rows[:, :half].reshape(group, cap, half)
        high = rows[:, half:].reshape(group, cap, half)
        send_buf[level, pl.ds(part * group, group)] = jnp.concatenate([low, high], axis=1).astype(bf16)

    def post(level, part):
        def go(turn, carry):
            halo_copy(level, turn).start()
            return carry

        lax.fori_loop(part * group, jnp.minimum((part + 1) * group, owners - 1), go, 0)

    for level in range(2):
        loads[2 + level].wait()
        if level == 0:
            fill(0, 0)
            pl.semaphore_wait(barrier, greeted)
            post(0, 0)

        def emit(part, carry):
            fill(level, part)
            post(level, part)
            return carry

        lax.fori_loop(1 - level, owners // group, emit, 0)
        halo_got[level, me] = send_buf[level, owners - 1]

    loads[4].wait()
    scatter[...] = jnp.where(iota((batch, batch), 0) == node_ids[...], 1.0, 0.0).astype(bf16)
    for part in range(batch // tile):
        ids = column(node_ids[:, part * tile : (part + 1) * tile])
        gather = jnp.where(ids == iota((tile, batch), 1), 1.0, 0.0).astype(bf16)
        h_start[part * tile : (part + 1) * tile] = dot(gather, hist[0]).astype(bf16)

    loads[5].wait()
    loads[6].wait()
    tiles[blocks * per_row] = jnp.zeros((tile, tile), bf16)

    def arrange(row, carry):
        down = pl.multiple_of(row * tile, tile)
        for block in range(all_blocks):
            index = blocks * per_row
            for t in range(per_row):
                index = jnp.where(cols[row, t] == block, row * per_row + t, index)
            values = tiles[index]
            adj[pl.ds(down, tile), block * tile : (block + 1) * tile] = values
            if block < batch_blocks:
                adj_back[block * tile : (block + 1) * tile, pl.ds(down, tile)] = values.astype(f32).T.astype(bf16)
        return carry

    lax.fori_loop(0, blocks, arrange, 0)

    def over_chunks(body):
        for part in range(chunks):
            body(pl.ds(part * chunk, chunk))

    def batch_part(source):
        def body(rows):
            partial[rows, :] = dot(adj[rows, :batch], source[...])

        over_chunks(body)

    def receive(level):
        span_wait(send_buf.at[level, pl.ds(0, owners - 1)], halo_recv.at[level])
        got = halo_got[level].astype(f32)
        low = got[:, :cap].reshape(slots, half)
        high = got[:, cap:].reshape(slots, half)
        halo[...] = jnp.concatenate([low, high], axis=1).astype(bf16)

    def preact(level, rows):
        summed = partial[rows, :] + dot(adj[rows, batch:], halo[...])
        mixed_rows = ((1.0 - RESTART) * summed + RESTART * h_start[rows, :].astype(f32)).astype(bf16)
        mixed[level, rows, :] = mixed_rows
        beta = layer_beta(level)
        return (1.0 - beta) * mixed_rows.astype(f32) + beta * dot(mixed_rows, weights[level])

    batch_part(h_start)
    loads[7].wait()
    receive(0)

    def first_layer(rows):
        z = preact(0, rows)
        sigma = jax.nn.sigmoid(z)
        hidden[rows, :] = (z * sigma).astype(bf16)
        slope[rows, :] = sigma * (1.0 + z * (1.0 - sigma))

    over_chunks(first_layer)
    batch_part(hidden)

    def write_back(rows):
        written_rows[rows, :] = dot(scatter[rows, :], hidden[...]).astype(bf16)

    over_chunks(write_back)
    store = pltpu.make_async_copy(written_rows, written.at[0], local_sems.at[len(loads)])
    store.start()
    mixed_turned[...] = mixed[0].astype(f32).T.astype(bf16)
    weight_turned[...] = weights[1].astype(f32).T.astype(bf16)
    loads[8].wait()
    receive(1)
    beta_last = layer_beta(1)

    def last_layer(rows):
        z = preact(1, rows)
        grad = (upstream[rows, :].astype(f32) * silu_slope(z)).astype(bf16)
        upstream[rows, :] = grad
        back[rows, :] = ((1.0 - beta_last) * grad.astype(f32) + beta_last * dot(grad, weight_turned[...])).astype(bf16)

    over_chunks(last_layer)
    source = sum_refs[0]
    source[width:, :] = (beta_last * dot_t(mixed[1], upstream[...])).astype(bf16)
    sum_send(grid, 1, *sum_refs)

    def first_grad(rows):
        total = dot(adj_back[rows, :], back[...])
        hidden[rows, :] = ((1.0 - RESTART) * total * slope[rows, :]).astype(bf16)

    over_chunks(first_grad)
    source[:width, :] = (layer_beta(0) * dot(mixed_turned[...], hidden[...])).astype(bf16)
    sum_send(grid, 0, *sum_refs)
    nodes_all = batch * owners * lax.axis_size("rep")
    sum_rest(grid, 1.0 / math.sqrt(nodes_all), total_out, *sum_refs)
    store.wait()
    for level in range(2):
        span_wait(send_buf.at[level, pl.ds(0, owners - 1)], halo_send.at[level])


def local(grid, history, tile_values, tile_cols, send_rows, send_count, node_ids, weights, upstream):
    levels, batch, width = history.shape
    blocks, per_row, tile, _ = tile_values.shape
    _, owners, cap = send_rows.shape
    slots = owners * cap
    bf16, f32 = jnp.bfloat16, jnp.float32
    vmem = pl.BlockSpec(memory_space=pltpu.VMEM)
    anywhere = pl.BlockSpec(memory_space=pl.ANY)
    written, total = pl.pallas_call(
        functools.partial(step_kernel, grid),
        out_shape=(jax.ShapeDtypeStruct((1, batch, width), bf16), jax.ShapeDtypeStruct((levels * width, width), bf16)),
        in_specs=[anywhere] * 8,
        out_specs=(anywhere, anywhere),
        scratch_shapes=[
            pltpu.SMEM((blocks, per_row), jnp.int32),
            pltpu.VMEM((cap, owners), jnp.int32),
            pltpu.VMEM((1, owners), jnp.int32),
            pltpu.VMEM((1, batch), jnp.int32),
            pltpu.VMEM((levels, width, width), bf16),
            pltpu.VMEM((batch, width), bf16),
            pltpu.VMEM((levels, batch, width), bf16),
            pltpu.VMEM((blocks * per_row + 1, tile, tile), bf16),
            pltpu.VMEM((batch, width), bf16),
            pltpu.VMEM((batch, batch + slots), bf16),
            pltpu.VMEM((batch, batch), bf16),
            pltpu.VMEM((slots, batch), bf16),
            pltpu.VMEM((batch, batch), bf16),
            pltpu.VMEM((batch, width), bf16),
            pltpu.VMEM((batch, width), bf16),
            pltpu.VMEM((batch, width), f32),
            pltpu.VMEM((levels, batch, width), bf16),
            pltpu.VMEM((batch, width), f32),
            pltpu.VMEM((batch, width), bf16),
            pltpu.VMEM((width, batch), bf16),
            pltpu.VMEM((width, width), bf16),
            pltpu.VMEM((levels, owners, 2 * cap, width // 2), bf16),
            pltpu.VMEM((levels, owners, 2 * cap, width // 2), bf16),
            pltpu.VMEM((slots, width), bf16),
            pltpu.SemaphoreType.DMA((10,)),
            pltpu.SemaphoreType.DMA((levels,)),
            pltpu.SemaphoreType.DMA((levels,)),
        ]
        + sum_scratch(grid, levels, width),
        compiler_params=pltpu.CompilerParams(collective_id=0, has_side_effects=True, vmem_limit_bytes=56 * 2**20),
    )(
        history,
        tile_values.reshape(blocks * per_row, tile, tile),
        tile_cols,
        send_rows[0].T,
        send_count,
        node_ids,
        weights,
        upstream,
    )

    def finish(written_ref, total_ref, written_out, total_out):
        written_out[...] = written_ref[...]
        for level in range(levels):
            total_out[level] = total_ref[level * width : (level + 1) * width].astype(f32)

    return pl.pallas_call(
        finish,
        out_shape=(jax.ShapeDtypeStruct(written.shape, bf16), jax.ShapeDtypeStruct((levels, width, width), f32)),
        in_specs=[vmem, vmem],
        out_specs=(vmem, vmem),
    )(written, total)


def solution(mesh):
    dom, rep = mesh.shape["dom"], mesh.shape["rep"]
    grid = (dom // RING, rep // 2, RING)
    return jax.shard_map(
        functools.partial(local, grid),
        mesh=mesh,
        in_specs=(
            P(None, ("dom", "rep"), None),
            P(("dom", "rep"), None, None, None),
            P(("dom", "rep"), None),
            P(("dom", "rep"), None, None),
            P(("dom", "rep"), None),
            P(("dom", "rep"), None),
            P(),
            P(("dom", "rep"), None),
        ),
        out_specs=(P(None, ("dom", "rep"), None), P()),
        check_vma=False,
    )
```

```python
import functools
import math

import jax
import jax.numpy as jnp
from jax import lax
from jax.experimental import pallas as pl
from jax.experimental.pallas import tpu as pltpu
from jax.sharding import PartitionSpec as P

RESTART = 0.1
RING = 16


def layer_beta(level):
    return math.log(0.5 / (level + 1) + 1.0)


def silu_slope(preact):
    sigma = jax.nn.sigmoid(preact)
    return sigma * (1.0 + preact * (1.0 - sigma))


MESH = pl.DeviceIdType.MESH


def span_wait(ref, sem):
    pltpu.make_async_copy(ref, ref, sem).wait()


def place(grid):
    nx, ny, nz = grid
    dom, rep = lax.axis_index("dom"), lax.axis_index("rep")
    return dom // nz, dom % nz, rep // 2, rep % 2


def far_first(n, turn):
    side = (turn + 1) // 2
    return (n // 2 + side * (1 - 2 * (turn % 2)) + n) % n


def ring_peer(grid, turn):
    nx, ny, nz = grid
    x, z, y, core = place(grid)
    return (x * nz + (z + far_first(nz, turn)) % nz, y * 2 + core)


def halo_peer(grid, turn):
    nx, ny, nz = grid
    x, z, y, core = place(grid)
    return ((x + far_first(nx, turn % nx)) % nx) * nz + (z + far_first(nz, turn // nx)) % nz


def greet(grid, barrier):
    nx, ny, nz = grid
    x, z, y, core = place(grid)
    rep, reps = lax.axis_index("rep"), 2 * ny

    def signal(target):
        pl.semaphore_signal(barrier, inc=1, device_id=target, device_id_type=MESH)

    def halo(turn, carry):
        signal((halo_peer(grid, turn), rep))
        return carry

    def layer(turn, carry):
        signal(((x + turn % nx) % nx * nz + z, (rep + 1 + turn // nx) % reps))
        return carry

    far = nx * nz // 2
    lax.fori_loop(0, far, halo, 0)
    lax.fori_loop(0, nx * (reps - 1), layer, 0)
    lax.fori_loop(far, nx * nz - 1, halo, 0)
    return nx * nz - 1 + nx * (reps - 1)


def link(stage, src, dst, target, send_sems, recv_sems):
    return pltpu.make_async_remote_copy(
        src_ref=src, dst_ref=dst, send_sem=send_sems.at[stage], recv_sem=recv_sems.at[stage], device_id=target, device_id_type=MESH
    )


def layer_share(grid, rows):
    nx, ny, nz = grid
    x, z, y, core = place(grid)
    reps = 2 * ny
    mine = x * reps + y * 2 + core

    def span(index):
        return pl.ds(pl.multiple_of(index * rows, rows), rows)

    def device(index):
        return (index // reps * nz + z, index % reps)

    return mine, span, device


def sum_send(grid, level, source, layer_got, ring_got, send_sems, recv_sems):
    shares, rows = layer_got.shape[0], layer_got.shape[1]
    group = shares // 2
    mine, span, device = layer_share(grid, rows)

    same = jnp.where(mine // group == level, 1, 0)

    def send(turn, carry):
        step = turn + 3
        step = jnp.where(step >= group - same, step - (group - same), step)
        index = level * group + (mine + same + step) % group
        link(0, source.at[span(index)], layer_got.at[mine], device(index), send_sems, recv_sems).start()
        return carry

    lax.fori_loop(0, group - same, send, 0)


def sum_rest(grid, scale, out, source, layer_got, ring_got, send_sems, recv_sems):
    nx, ny, nz = grid
    shares, rows = layer_got.shape[0], layer_got.shape[1]
    mine, span, device = layer_share(grid, rows)
    x, z, y, core = place(grid)
    layer_got[mine] = source[span(mine), :]
    span_wait(layer_got.at[pl.ds(0, shares - 1)], recv_sems.at[0])
    ring_got[z] = jnp.sum(layer_got[...].astype(jnp.float32), axis=0).astype(jnp.bfloat16)

    def ring_send(turn, carry):
        link(1, ring_got.at[z], ring_got.at[z], ring_peer(grid, turn), send_sems, recv_sems).start()
        return carry

    lax.fori_loop(0, nz - 1, ring_send, 0, unroll=nz - 1)
    span_wait(source.at[pl.ds(0, (shares - 1) * rows)], send_sems.at[0])
    span_wait(ring_got.at[pl.ds(0, nz - 1)], recv_sems.at[1])
    total = jnp.sum(ring_got[...].astype(jnp.float32), axis=0) * scale
    source[span(mine), :] = total.astype(jnp.bfloat16)

    def share(turn, carry):
        over_x = (x + far_first(nx, turn // (2 * ny))) % nx
        over_y = (y + far_first(ny, turn // 2 % ny)) % ny
        index = (over_x * ny + over_y) * 2 + (core + 1 + turn) % 2
        link(2, source.at[span(mine)], out.at[span(mine)], device(index), send_sems, recv_sems).start()
        return carry

    lax.fori_loop(0, shares - 1, share, 0, unroll=shares - 1)
    own = pltpu.make_async_copy(source.at[span(mine)], out.at[span(mine)], send_sems.at[3])
    own.start()
    span_wait(ring_got.at[pl.ds(0, nz - 1)], send_sems.at[1])
    span_wait(source.at[pl.ds(0, (shares - 1) * rows)], send_sems.at[2])
    own.wait()
    span_wait(source.at[pl.ds(0, (shares - 1) * rows)], recv_sems.at[2])


def sum_scratch(grid, levels, side):
    nx, ny, nz = grid
    shares = nx * ny * 2
    rows = levels * side // shares
    return [
        pltpu.VMEM((levels * side, side), jnp.bfloat16),
        pltpu.VMEM((shares, rows, side), jnp.bfloat16),
        pltpu.VMEM((nz, rows, side), jnp.bfloat16),
        pltpu.SemaphoreType.DMA((4,)),
        pltpu.SemaphoreType.DMA((3,)),
    ]


def dot(a, b):
    return jnp.dot(a, b, preferred_element_type=jnp.float32)


def iota(shape, axis):
    return lax.broadcasted_iota(jnp.int32, shape, axis)


def column(row):
    n = row.shape[1]
    picked = jnp.where(iota((n, n), 0) == iota((n, n), 1), jnp.broadcast_to(row, (n, n)), 0)
    return jnp.sum(picked, axis=1, keepdims=True)


def step_kernel(
    grid,
    history,
    tiles_hbm,
    cols_hbm,
    send_rows_hbm,
    send_count_hbm,
    node_ids_hbm,
    weights_hbm,
    upstream_hbm,
    written,
    total_out,
    cols,
    send_rows,
    send_count,
    node_ids,
    weights,
    written_rows,
    hist,
    tiles,
    upstream,
    adj,
    adj_back,
    picker,
    scatter,
    h_start,
    hidden,
    partial,
    mixed,
    slope,
    back,
    mixed_turned,
    last_turned,
    weight_turned,
    send_buf,
    halo_got,
    halo,
    local_sems,
    halo_send,
    halo_recv,
    *sum_refs,
):
    nx, ny, nz = grid
    bf16, f32 = jnp.bfloat16, jnp.float32
    batch, width = hist.shape[1], hist.shape[2]
    half = width // 2
    tile = tiles.shape[1]
    blocks, per_row = cols.shape
    batch_blocks = batch // tile
    all_blocks = adj.shape[1] // tile
    cap, owners = send_rows.shape
    chunk = min(512, batch)
    chunks = batch // chunk
    me = lax.axis_index("dom")

    barrier = pltpu.get_barrier_semaphore()
    loads = [
        pltpu.make_async_copy(src, dst, local_sems.at[order])
        for order, (src, dst) in enumerate(
            [
                (send_rows_hbm, send_rows),
                (send_count_hbm, send_count),
                (history.at[0], hist.at[0]),
                (history.at[1], hist.at[1]),
                (node_ids_hbm, node_ids),
                (cols_hbm, cols),
                (tiles_hbm, tiles.at[pl.ds(0, blocks * per_row)]),
                (weights_hbm, weights),
                (upstream_hbm, upstream),
            ]
        )
    ]
    for load in loads[:3]:
        load.start()
    greeted = greet(grid, barrier)
    for load in loads[3:]:
        load.start()
    for load in loads[:2]:
        load.wait()

    slots = owners * cap
    slot = iota((slots, 1), 0)
    peer = halo_peer(grid, slot // cap)
    turn = (peer == iota((slots, owners), 1)).astype(f32)
    listed = lax.dot_general(
        turn, send_rows[...].astype(f32), (((1,), (1,)), ((), ())), precision=lax.Precision.HIGHEST, preferred_element_type=f32
    )
    listed = jnp.sum(jnp.where(iota((slots, cap), 1) == slot % cap, listed, 0.0), axis=1, keepdims=True)
    count = jnp.sum(turn * send_count[...].astype(f32), axis=1, keepdims=True)
    wanted = jnp.where((slot % cap).astype(f32) < count, listed, -1.0)
    picker[...] = jnp.where(wanted == iota((slots, batch), 1).astype(f32), 1.0, 0.0).astype(bf16)

    group = max(1, 128 // cap)

    def halo_copy(level, turn):
        return pltpu.make_async_remote_copy(
            src_ref=send_buf.at[level, turn],
            dst_ref=halo_got.at[level, me],
            send_sem=halo_send.at[level],
            recv_sem=halo_recv.at[level],
            device_id=(halo_peer(grid, turn), lax.axis_index("rep")),
            device_id_type=MESH,
        )

    def fill(level, part):
        start = pl.multiple_of(part * group * cap, group * cap)
        rows = dot(picker[pl.ds(start, group * cap), :], hist[level])
        low = rows[:, :half].reshape(group, cap, half)
        high = rows[:, half:].reshape(group, cap, half)
        send_buf[level, pl.ds(part * group, group)] = jnp.concatenate([low, high], axis=1).astype(bf16)

    def post(level, part):
        def go(turn, carry):
            halo_copy(level, turn).start()
            return carry

        lax.fori_loop(part * group, jnp.minimum((part + 1) * group, owners - 1), go, 0)

    for level in range(2):
        loads[2 + level].wait()
        if level == 0:
            fill(0, 0)
            pl.semaphore_wait(barrier, greeted)
            post(0, 0)

        def emit(part, carry):
            fill(level, part)
            post(level, part)
            return carry

        lax.fori_loop(1 - level, owners // group, emit, 0)
        halo_got[level, me] = send_buf[level, owners - 1]

    loads[4].wait()
    scatter[...] = jnp.where(iota((batch, batch), 0) == node_ids[...], 1.0, 0.0).astype(bf16)
    for part in range(batch // tile):
        ids = column(node_ids[:, part * tile : (part + 1) * tile])
        gather = jnp.where(ids == iota((tile, batch), 1), 1.0, 0.0).astype(bf16)
        h_start[part * tile : (part + 1) * tile] = dot(gather, hist[0]).astype(bf16)

    loads[5].wait()
    loads[6].wait()
    tiles[blocks * per_row] = jnp.zeros((tile, tile), bf16)

    def arrange(row, carry):
        down = pl.multiple_of(row * tile, tile)
        for block in range(all_blocks):
            index = blocks * per_row
            for t in range(per_row):
                index = jnp.where(cols[row, t] == block, row * per_row + t, index)
            values = tiles[index]
            adj[pl.ds(down, tile), block * tile : (block + 1) * tile] = values
            if block < batch_blocks:
                adj_back[block * tile : (block + 1) * tile, pl.ds(down, tile)] = values.astype(f32).T.astype(bf16)
        return carry

    lax.fori_loop(0, blocks, arrange, 0)

    def over_chunks(body):
        for part in range(chunks):
            body(pl.ds(part * chunk, chunk))

    def batch_part(source):
        def body(rows):
            partial[rows, :] = dot(adj[rows, :batch], source[...])

        over_chunks(body)

    def receive(level):
        span_wait(send_buf.at[level, pl.ds(0, owners - 1)], halo_recv.at[level])
        got = halo_got[level].astype(f32)
        low = got[:, :cap].reshape(slots, half)
        high = got[:, cap:].reshape(slots, half)
        halo[...] = jnp.concatenate([low, high], axis=1).astype(bf16)

    def preact(level, rows):
        summed = partial[rows, :] + dot(adj[rows, batch:], halo[...])
        mixed_rows = ((1.0 - RESTART) * summed + RESTART * h_start[rows, :].astype(f32)).astype(bf16)
        mixed[level, rows, :] = mixed_rows
        beta = layer_beta(level)
        return (1.0 - beta) * mixed_rows.astype(f32) + beta * dot(mixed_rows, weights[level])

    batch_part(h_start)
    loads[7].wait()
    receive(0)

    def first_layer(rows):
        z = preact(0, rows)
        sigma = jax.nn.sigmoid(z)
        hidden[rows, :] = (z * sigma).astype(bf16)
        slope[rows, :] = sigma * (1.0 + z * (1.0 - sigma))

    over_chunks(first_layer)
    batch_part(hidden)

    def write_back(rows):
        written_rows[rows, :] = dot(scatter[rows, :], hidden[...]).astype(bf16)

    over_chunks(write_back)
    store = pltpu.make_async_copy(written_rows, written.at[0], local_sems.at[len(loads)])
    store.start()
    mixed_turned[...] = mixed[0].astype(f32).T.astype(bf16)
    weight_turned[...] = weights[1].astype(f32).T.astype(bf16)
    loads[8].wait()
    receive(1)
    beta_last = layer_beta(1)

    def last_layer(rows):
        z = preact(1, rows)
        last_turned[:, rows] = mixed[1, rows, :].astype(f32).T.astype(bf16)
        grad = (upstream[rows, :].astype(f32) * silu_slope(z)).astype(bf16)
        upstream[rows, :] = grad
        back[rows, :] = ((1.0 - beta_last) * grad.astype(f32) + beta_last * dot(grad, weight_turned[...])).astype(bf16)

    over_chunks(last_layer)
    source = sum_refs[0]
    source[width:, :] = (beta_last * dot(last_turned[...], upstream[...])).astype(bf16)
    sum_send(grid, 1, *sum_refs)

    def first_grad(rows):
        total = dot(adj_back[rows, :], back[...])
        hidden[rows, :] = ((1.0 - RESTART) * total * slope[rows, :]).astype(bf16)

    over_chunks(first_grad)
    source[:width, :] = (layer_beta(0) * dot(mixed_turned[...], hidden[...])).astype(bf16)
    sum_send(grid, 0, *sum_refs)
    nodes_all = batch * owners * lax.axis_size("rep")
    sum_rest(grid, 1.0 / math.sqrt(nodes_all), total_out, *sum_refs)
    store.wait()
    for level in range(2):
        span_wait(send_buf.at[level, pl.ds(0, owners - 1)], halo_send.at[level])


def local(grid, history, tile_values, tile_cols, send_rows, send_count, node_ids, weights, upstream):
    levels, batch, width = history.shape
    blocks, per_row, tile, _ = tile_values.shape
    _, owners, cap = send_rows.shape
    slots = owners * cap
    bf16, f32 = jnp.bfloat16, jnp.float32
    vmem = pl.BlockSpec(memory_space=pltpu.VMEM)
    anywhere = pl.BlockSpec(memory_space=pl.ANY)
    written, total = pl.pallas_call(
        functools.partial(step_kernel, grid),
        out_shape=(jax.ShapeDtypeStruct((1, batch, width), bf16), jax.ShapeDtypeStruct((levels * width, width), bf16)),
        in_specs=[anywhere] * 8,
        out_specs=(anywhere, anywhere),
        scratch_shapes=[
            pltpu.SMEM((blocks, per_row), jnp.int32),
            pltpu.VMEM((cap, owners), jnp.int32),
            pltpu.VMEM((1, owners), jnp.int32),
            pltpu.VMEM((1, batch), jnp.int32),
            pltpu.VMEM((levels, width, width), bf16),
            pltpu.VMEM((batch, width), bf16),
            pltpu.VMEM((levels, batch, width), bf16),
            pltpu.VMEM((blocks * per_row + 1, tile, tile), bf16),
            pltpu.VMEM((batch, width), bf16),
            pltpu.VMEM((batch, batch + slots), bf16),
            pltpu.VMEM((batch, batch), bf16),
            pltpu.VMEM((slots, batch), bf16),
            pltpu.VMEM((batch, batch), bf16),
            pltpu.VMEM((batch, width), bf16),
            pltpu.VMEM((batch, width), bf16),
            pltpu.VMEM((batch, width), f32),
            pltpu.VMEM((levels, batch, width), bf16),
            pltpu.VMEM((batch, width), f32),
            pltpu.VMEM((batch, width), bf16),
            pltpu.VMEM((width, batch), bf16),
            pltpu.VMEM((width, batch), bf16),
            pltpu.VMEM((width, width), bf16),
            pltpu.VMEM((levels, owners, 2 * cap, width // 2), bf16),
            pltpu.VMEM((levels, owners, 2 * cap, width // 2), bf16),
            pltpu.VMEM((slots, width), bf16),
            pltpu.SemaphoreType.DMA((10,)),
            pltpu.SemaphoreType.DMA((levels,)),
            pltpu.SemaphoreType.DMA((levels,)),
        ]
        + sum_scratch(grid, levels, width),
        compiler_params=pltpu.CompilerParams(collective_id=0, has_side_effects=True, vmem_limit_bytes=56 * 2**20),
    )(
        history,
        tile_values.reshape(blocks * per_row, tile, tile),
        tile_cols,
        send_rows[0].T,
        send_count,
        node_ids,
        weights,
        upstream,
    )

    def finish(written_ref, total_ref, written_out, total_out):
        written_out[...] = written_ref[...]
        for level in range(levels):
            total_out[level] = total_ref[level * width : (level + 1) * width].astype(f32)

    return pl.pallas_call(
        finish,
        out_shape=(jax.ShapeDtypeStruct(written.shape, bf16), jax.ShapeDtypeStruct((levels, width, width), f32)),
        in_specs=[vmem, vmem],
        out_specs=(vmem, vmem),
    )(written, total)


def solution(mesh):
    dom, rep = mesh.shape["dom"], mesh.shape["rep"]
    grid = (dom // RING, rep // 2, RING)
    return jax.shard_map(
        functools.partial(local, grid),
        mesh=mesh,
        in_specs=(
            P(None, ("dom", "rep"), None),
            P(("dom", "rep"), None, None, None),
            P(("dom", "rep"), None),
            P(("dom", "rep"), None, None),
            P(("dom", "rep"), None),
            P(("dom", "rep"), None),
            P(),
            P(("dom", "rep"), None),
        ),
        out_specs=(P(None, ("dom", "rep"), None), P()),
        check_vma=False,
    )
```

```python
import functools
import math

import jax
import jax.numpy as jnp
from jax import lax
from jax.experimental import pallas as pl
from jax.experimental.pallas import tpu as pltpu
from jax.sharding import PartitionSpec as P

RESTART = 0.1
RING = 16


def layer_beta(level):
    return math.log(0.5 / (level + 1) + 1.0)


def silu_slope(preact):
    sigma = jax.nn.sigmoid(preact)
    return sigma * (1.0 + preact * (1.0 - sigma))


MESH = pl.DeviceIdType.MESH


def span_wait(ref, sem):
    pltpu.make_async_copy(ref, ref, sem).wait()


def place(grid):
    nx, ny, nz = grid
    dom, rep = lax.axis_index("dom"), lax.axis_index("rep")
    return dom // nz, dom % nz, rep // 2, rep % 2


def far_first(n, turn):
    side = (turn + 1) // 2
    return (n // 2 + side * (1 - 2 * (turn % 2)) + n) % n


def ring_peer(grid, turn):
    nx, ny, nz = grid
    x, z, y, core = place(grid)
    return (x * nz + (z + far_first(nz, turn)) % nz, y * 2 + core)


def halo_peer(grid, turn):
    nx, ny, nz = grid
    x, z, y, core = place(grid)
    return ((x + far_first(nx, turn % nx)) % nx) * nz + (z + far_first(nz, turn // nx)) % nz


def greet(grid, barrier):
    nx, ny, nz = grid
    x, z, y, core = place(grid)
    rep, reps = lax.axis_index("rep"), 2 * ny

    def signal(target):
        pl.semaphore_signal(barrier, inc=1, device_id=target, device_id_type=MESH)

    def halo(turn, carry):
        signal((halo_peer(grid, turn), rep))
        return carry

    def layer(turn, carry):
        signal(((x + turn % nx) % nx * nz + z, (rep + 1 + turn // nx) % reps))
        return carry

    far = nx * nz // 2
    lax.fori_loop(0, far, halo, 0)
    lax.fori_loop(0, nx * (reps - 1), layer, 0)
    lax.fori_loop(far, nx * nz - 1, halo, 0)
    return nx * nz - 1 + nx * (reps - 1)


def link(stage, src, dst, target, send_sems, recv_sems):
    return pltpu.make_async_remote_copy(
        src_ref=src, dst_ref=dst, send_sem=send_sems.at[stage], recv_sem=recv_sems.at[stage], device_id=target, device_id_type=MESH
    )


def layer_share(grid, rows):
    nx, ny, nz = grid
    x, z, y, core = place(grid)
    reps = 2 * ny
    mine = x * reps + y * 2 + core

    def span(index):
        return pl.ds(pl.multiple_of(index * rows, rows), rows)

    def device(index):
        return (index // reps * nz + z, index % reps)

    return mine, span, device


def sum_send(grid, level, source, layer_got, ring_got, send_sems, recv_sems):
    shares, rows = layer_got.shape[0], layer_got.shape[1]
    group = shares // 2
    mine, span, device = layer_share(grid, rows)

    same = jnp.where(mine // group == level, 1, 0)

    def send(turn, carry):
        step = turn + 3
        step = jnp.where(step >= group - same, step - (group - same), step)
        index = level * group + (mine + same + step) % group
        link(0, source.at[span(index)], layer_got.at[mine], device(index), send_sems, recv_sems).start()
        return carry

    lax.fori_loop(0, group - same, send, 0)


def sum_rest(grid, scale, out, source, layer_got, ring_got, send_sems, recv_sems):
    nx, ny, nz = grid
    shares, rows = layer_got.shape[0], layer_got.shape[1]
    mine, span, device = layer_share(grid, rows)
    x, z, y, core = place(grid)
    layer_got[mine] = source[span(mine), :]
    span_wait(layer_got.at[pl.ds(0, shares - 1)], recv_sems.at[0])
    ring_got[z] = jnp.sum(layer_got[...].astype(jnp.float32), axis=0).astype(jnp.bfloat16)

    def ring_send(turn, carry):
        link(1, ring_got.at[z], ring_got.at[z], ring_peer(grid, turn), send_sems, recv_sems).start()
        return carry

    lax.fori_loop(0, nz - 1, ring_send, 0, unroll=nz - 1)
    span_wait(source.at[pl.ds(0, (shares - 1) * rows)], send_sems.at[0])
    span_wait(ring_got.at[pl.ds(0, nz - 1)], recv_sems.at[1])
    total = jnp.sum(ring_got[...].astype(jnp.float32), axis=0) * scale
    source[span(mine), :] = total.astype(jnp.bfloat16)

    def share(turn, carry):
        over_x = (x + far_first(nx, turn // (2 * ny))) % nx
        over_y = (y + far_first(ny, turn // 2 % ny)) % ny
        index = (over_x * ny + over_y) * 2 + (core + 1 + turn) % 2
        link(2, source.at[span(mine)], out.at[span(mine)], device(index), send_sems, recv_sems).start()
        return carry

    lax.fori_loop(0, shares - 1, share, 0, unroll=shares - 1)
    own = pltpu.make_async_copy(source.at[span(mine)], out.at[span(mine)], send_sems.at[3])
    own.start()
    span_wait(ring_got.at[pl.ds(0, nz - 1)], send_sems.at[1])
    span_wait(source.at[pl.ds(0, (shares - 1) * rows)], send_sems.at[2])
    own.wait()
    span_wait(source.at[pl.ds(0, (shares - 1) * rows)], recv_sems.at[2])


def sum_scratch(grid, levels, side):
    nx, ny, nz = grid
    shares = nx * ny * 2
    rows = levels * side // shares
    return [
        pltpu.VMEM((levels * side, side), jnp.bfloat16),
        pltpu.VMEM((shares, rows, side), jnp.bfloat16),
        pltpu.VMEM((nz, rows, side), jnp.bfloat16),
        pltpu.SemaphoreType.DMA((4,)),
        pltpu.SemaphoreType.DMA((3,)),
    ]


def dot(a, b):
    return jnp.dot(a, b, preferred_element_type=jnp.float32)


def iota(shape, axis):
    return lax.broadcasted_iota(jnp.int32, shape, axis)


def column(row):
    n = row.shape[1]
    picked = jnp.where(iota((n, n), 0) == iota((n, n), 1), jnp.broadcast_to(row, (n, n)), 0)
    return jnp.sum(picked, axis=1, keepdims=True)


def step_kernel(
    grid,
    history,
    tiles_hbm,
    cols_hbm,
    send_rows_hbm,
    send_count_hbm,
    node_ids_hbm,
    weights_hbm,
    upstream_hbm,
    written,
    total_out,
    cols,
    send_rows,
    send_count,
    node_ids,
    weights,
    written_rows,
    hist,
    tiles,
    upstream,
    adj,
    adj_back,
    picker,
    scatter,
    h_start,
    hidden,
    partial,
    mixed,
    slope,
    back,
    mixed_turned,
    last_turned,
    weight_turned,
    send_buf,
    halo_got,
    halo,
    local_sems,
    halo_send,
    halo_recv,
    *sum_refs,
):
    nx, ny, nz = grid
    bf16, f32 = jnp.bfloat16, jnp.float32
    batch, width = hist.shape[1], hist.shape[2]
    half = width // 2
    tile = tiles.shape[1]
    blocks, per_row = cols.shape
    batch_blocks = batch // tile
    all_blocks = adj.shape[1] // tile
    cap, owners = send_rows.shape
    chunk = min(512, batch)
    chunks = batch // chunk
    me = lax.axis_index("dom")

    barrier = pltpu.get_barrier_semaphore()
    loads = [
        pltpu.make_async_copy(src, dst, local_sems.at[order])
        for order, (src, dst) in enumerate(
            [
                (send_rows_hbm, send_rows),
                (send_count_hbm, send_count),
                (history.at[0], hist.at[0]),
                (history.at[1], hist.at[1]),
                (node_ids_hbm, node_ids),
                (cols_hbm, cols),
                (tiles_hbm, tiles.at[pl.ds(0, blocks * per_row)]),
                (weights_hbm, weights),
                (upstream_hbm, upstream),
            ]
        )
    ]
    for load in loads[:3]:
        load.start()
    greeted = greet(grid, barrier)
    for load in loads[3:]:
        load.start()
    for load in loads[:2]:
        load.wait()

    slots = owners * cap
    slot = iota((slots, 1), 0)
    peer = halo_peer(grid, slot // cap)
    turn = (peer == iota((slots, owners), 1)).astype(f32)
    listed = lax.dot_general(
        turn, send_rows[...].astype(f32), (((1,), (1,)), ((), ())), precision=lax.Precision.HIGHEST, preferred_element_type=f32
    )
    listed = jnp.sum(jnp.where(iota((slots, cap), 1) == slot % cap, listed, 0.0), axis=1, keepdims=True)
    count = jnp.sum(turn * send_count[...].astype(f32), axis=1, keepdims=True)
    wanted = jnp.where((slot % cap).astype(f32) < count, listed, -1.0)
    picker[...] = jnp.where(wanted == iota((slots, batch), 1).astype(f32), 1.0, 0.0).astype(bf16)

    group = max(1, 128 // cap)

    def halo_copy(level, turn):
        return pltpu.make_async_remote_copy(
            src_ref=send_buf.at[level, turn],
            dst_ref=halo_got.at[level, me],
            send_sem=halo_send.at[level],
            recv_sem=halo_recv.at[level],
            device_id=(halo_peer(grid, turn), lax.axis_index("rep")),
            device_id_type=MESH,
        )

    def fill(level, part):
        start = pl.multiple_of(part * group * cap, group * cap)
        rows = dot(picker[pl.ds(start, group * cap), :], hist[level])
        low = rows[:, :half].reshape(group, cap, half)
        high = rows[:, half:].reshape(group, cap, half)
        send_buf[level, pl.ds(part * group, group)] = jnp.concatenate([low, high], axis=1).astype(bf16)

    def post(level, part):
        def go(turn, carry):
            halo_copy(level, turn).start()
            return carry

        lax.fori_loop(part * group, jnp.minimum((part + 1) * group, owners - 1), go, 0)

    for level in range(2):
        loads[2 + level].wait()
        if level == 0:
            lax.fori_loop(0, owners // group, lambda part, carry: (fill(0, part), carry)[1], 0)
            pl.semaphore_wait(barrier, greeted)

        def emit(part, carry):
            if level > 0:
                fill(level, part)
            post(level, part)
            return carry

        lax.fori_loop(0, owners // group, emit, 0)
        halo_got[level, me] = send_buf[level, owners - 1]

    loads[4].wait()
    scatter[...] = jnp.where(iota((batch, batch), 0) == node_ids[...], 1.0, 0.0).astype(bf16)
    for part in range(batch // tile):
        ids = column(node_ids[:, part * tile : (part + 1) * tile])
        gather = jnp.where(ids == iota((tile, batch), 1), 1.0, 0.0).astype(bf16)
        h_start[part * tile : (part + 1) * tile] = dot(gather, hist[0]).astype(bf16)

    loads[5].wait()
    loads[6].wait()
    tiles[blocks * per_row] = jnp.zeros((tile, tile), bf16)

    def arrange(row, carry):
        down = pl.multiple_of(row * tile, tile)
        for block in range(all_blocks):
            index = blocks * per_row
            for t in range(per_row):
                index = jnp.where(cols[row, t] == block, row * per_row + t, index)
            values = tiles[index]
            adj[pl.ds(down, tile), block * tile : (block + 1) * tile] = values
            if block < batch_blocks:
                adj_back[block * tile : (block + 1) * tile, pl.ds(down, tile)] = values.astype(f32).T.astype(bf16)
        return carry

    lax.fori_loop(0, blocks, arrange, 0)

    def over_chunks(body):
        for part in range(chunks):
            body(pl.ds(part * chunk, chunk))

    def batch_part(source):
        def body(rows):
            partial[rows, :] = dot(adj[rows, :batch], source[...])

        over_chunks(body)

    def receive(level):
        span_wait(send_buf.at[level, pl.ds(0, owners - 1)], halo_recv.at[level])
        got = halo_got[level].astype(f32)
        low = got[:, :cap].reshape(slots, half)
        high = got[:, cap:].reshape(slots, half)
        halo[...] = jnp.concatenate([low, high], axis=1).astype(bf16)

    def preact(level, rows):
        summed = partial[rows, :] + dot(adj[rows, batch:], halo[...])
        mixed_rows = ((1.0 - RESTART) * summed + RESTART * h_start[rows, :].astype(f32)).astype(bf16)
        mixed[level, rows, :] = mixed_rows
        beta = layer_beta(level)
        return (1.0 - beta) * mixed_rows.astype(f32) + beta * dot(mixed_rows, weights[level])

    batch_part(h_start)
    loads[7].wait()
    receive(0)

    def first_layer(rows):
        z = preact(0, rows)
        sigma = jax.nn.sigmoid(z)
        hidden[rows, :] = (z * sigma).astype(bf16)
        slope[rows, :] = sigma * (1.0 + z * (1.0 - sigma))

    over_chunks(first_layer)
    batch_part(hidden)

    def write_back(rows):
        written_rows[rows, :] = dot(scatter[rows, :], hidden[...]).astype(bf16)

    over_chunks(write_back)
    store = pltpu.make_async_copy(written_rows, written.at[0], local_sems.at[len(loads)])
    store.start()
    mixed_turned[...] = mixed[0].astype(f32).T.astype(bf16)
    weight_turned[...] = weights[1].astype(f32).T.astype(bf16)
    loads[8].wait()
    receive(1)
    beta_last = layer_beta(1)

    def last_layer(rows):
        z = preact(1, rows)
        last_turned[:, rows] = mixed[1, rows, :].astype(f32).T.astype(bf16)
        grad = (upstream[rows, :].astype(f32) * silu_slope(z)).astype(bf16)
        upstream[rows, :] = grad
        back[rows, :] = ((1.0 - beta_last) * grad.astype(f32) + beta_last * dot(grad, weight_turned[...])).astype(bf16)

    over_chunks(last_layer)
    source = sum_refs[0]
    source[width:, :] = (beta_last * dot(last_turned[...], upstream[...])).astype(bf16)
    sum_send(grid, 1, *sum_refs)

    def first_grad(rows):
        total = dot(adj_back[rows, :], back[...])
        hidden[rows, :] = ((1.0 - RESTART) * total * slope[rows, :]).astype(bf16)

    over_chunks(first_grad)
    source[:width, :] = (layer_beta(0) * dot(mixed_turned[...], hidden[...])).astype(bf16)
    sum_send(grid, 0, *sum_refs)
    nodes_all = batch * owners * lax.axis_size("rep")
    sum_rest(grid, 1.0 / math.sqrt(nodes_all), total_out, *sum_refs)
    store.wait()
    for level in range(2):
        span_wait(send_buf.at[level, pl.ds(0, owners - 1)], halo_send.at[level])


def local(grid, history, tile_values, tile_cols, send_rows, send_count, node_ids, weights, upstream):
    levels, batch, width = history.shape
    blocks, per_row, tile, _ = tile_values.shape
    _, owners, cap = send_rows.shape
    slots = owners * cap
    bf16, f32 = jnp.bfloat16, jnp.float32
    vmem = pl.BlockSpec(memory_space=pltpu.VMEM)
    anywhere = pl.BlockSpec(memory_space=pl.ANY)
    written, total = pl.pallas_call(
        functools.partial(step_kernel, grid),
        out_shape=(jax.ShapeDtypeStruct((1, batch, width), bf16), jax.ShapeDtypeStruct((levels * width, width), bf16)),
        in_specs=[anywhere] * 8,
        out_specs=(anywhere, anywhere),
        scratch_shapes=[
            pltpu.SMEM((blocks, per_row), jnp.int32),
            pltpu.VMEM((cap, owners), jnp.int32),
            pltpu.VMEM((1, owners), jnp.int32),
            pltpu.VMEM((1, batch), jnp.int32),
            pltpu.VMEM((levels, width, width), bf16),
            pltpu.VMEM((batch, width), bf16),
            pltpu.VMEM((levels, batch, width), bf16),
            pltpu.VMEM((blocks * per_row + 1, tile, tile), bf16),
            pltpu.VMEM((batch, width), bf16),
            pltpu.VMEM((batch, batch + slots), bf16),
            pltpu.VMEM((batch, batch), bf16),
            pltpu.VMEM((slots, batch), bf16),
            pltpu.VMEM((batch, batch), bf16),
            pltpu.VMEM((batch, width), bf16),
            pltpu.VMEM((batch, width), bf16),
            pltpu.VMEM((batch, width), f32),
            pltpu.VMEM((levels, batch, width), bf16),
            pltpu.VMEM((batch, width), f32),
            pltpu.VMEM((batch, width), bf16),
            pltpu.VMEM((width, batch), bf16),
            pltpu.VMEM((width, batch), bf16),
            pltpu.VMEM((width, width), bf16),
            pltpu.VMEM((levels, owners, 2 * cap, width // 2), bf16),
            pltpu.VMEM((levels, owners, 2 * cap, width // 2), bf16),
            pltpu.VMEM((slots, width), bf16),
            pltpu.SemaphoreType.DMA((10,)),
            pltpu.SemaphoreType.DMA((levels,)),
            pltpu.SemaphoreType.DMA((levels,)),
        ]
        + sum_scratch(grid, levels, width),
        compiler_params=pltpu.CompilerParams(collective_id=0, has_side_effects=True, vmem_limit_bytes=56 * 2**20),
    )(
        history,
        tile_values.reshape(blocks * per_row, tile, tile),
        tile_cols,
        send_rows[0].T,
        send_count,
        node_ids,
        weights,
        upstream,
    )

    def finish(written_ref, total_ref, written_out, total_out):
        written_out[...] = written_ref[...]
        for level in range(levels):
            total_out[level] = total_ref[level * width : (level + 1) * width].astype(f32)

    return pl.pallas_call(
        finish,
        out_shape=(jax.ShapeDtypeStruct(written.shape, bf16), jax.ShapeDtypeStruct((levels, width, width), f32)),
        in_specs=[vmem, vmem],
        out_specs=(vmem, vmem),
    )(written, total)


def solution(mesh):
    dom, rep = mesh.shape["dom"], mesh.shape["rep"]
    grid = (dom // RING, rep // 2, RING)
    return jax.shard_map(
        functools.partial(local, grid),
        mesh=mesh,
        in_specs=(
            P(None, ("dom", "rep"), None),
            P(("dom", "rep"), None, None, None),
            P(("dom", "rep"), None),
            P(("dom", "rep"), None, None),
            P(("dom", "rep"), None),
            P(("dom", "rep"), None),
            P(),
            P(("dom", "rep"), None),
        ),
        out_specs=(P(None, ("dom", "rep"), None), P()),
        check_vma=False,
    )
```
